128 devices in a mesh: lat: 16 (over y, z_lo, core), lon: 8 (over x, z_hi).
Axes of the slice: x: 4, y: 4, z: 4 (z_hi: 2, z_lo: 2; z = z_hi * 2 + z_lo), core: 2. Of those that a mesh axis runs over, the one named last changes fastest.
Arguments:
- fields: bfloat16 [128, 720, 6400], P(None, 'lon', 'lat'), may hold values from -6 to 6
- surf_weight: bfloat16 [4, 100, 512], replicated, may hold values from -0.625 to 0.625
- atmos_weight: bfloat16 [5, 100, 512], replicated, may hold values from -0.625 to 0.625
- level_bias_table: float32 [12, 512], replicated, may hold values from -6 to 6
- latents: bfloat16 [3, 512], replicated, may hold values from -6 to 6
- query_matrix: bfloat16 [512, 512], replicated, as said below
- key_weight: bfloat16 [512, 512], replicated, may hold values from -0.25 to 0.25
- value_weight: bfloat16 [512, 512], replicated, may hold values from -0.25 to 0.25
- out_weight: bfloat16 [512, 512], replicated, may hold values from -0.25 to 0.25
Outputs:
- encoded: bfloat16 [128, 720, 4, 512], P('lat', 'lon')
The draws below stay inside these ranges and needn't reach their ends.
Inputs may be any that keep to these rules, and one draw needn't show every extreme that they name: `query_matrix`: entries of either sign, independent.
All inputs are finite; a program needn't handle non-finite values.
Results may differ from the reference program's by a relative error of at most 0.012.
The reference program's roundings to bfloat16 on the way count: a program that leaves them out, or rounds other values in their place, can miss the bound.
Values may be sent and summed in bfloat16 or wider, within the bound.
A program may use at most 192 MiB of HBM per device.

```python
import math
import jax
import jax.numpy as jnp
from jax import lax

C = 512
HEADS = 16
HEAD_CHANNELS = 32
PATCH = 10
NSURF = 4
NATM = 5
LATENT = 3
LEV = 12
F = 64
LONGITUDE_TOKENS = 720
LAT_TOK = 128


def draw_query_matrix(key, part):
    key = jax.random.fold_in(key, 5)
    values_drawn = jax.random.truncated_normal(key, -3.0, 3.0, (C, C), jnp.float32) / math.sqrt(C)
    return values_drawn.astype(jnp.bfloat16)


def block_scale(stream_key, dims, cuts, smallest, high):
    level = 1.0
    for axis_at, shards_of in cuts:
        heights = jax.random.uniform(jax.random.fold_in(jax.random.fold_in(stream_key, 6), axis_at), (shards_of,), jnp.float32, smallest / len(cuts), high / len(cuts))
        level = level * jnp.repeat(jnp.exp(heights), dims[axis_at] // shards_of).reshape((-1,) + (1,) * (len(dims) - 1 - axis_at))
    return level


def scatter_about(stream_key, extent, scale, bound, pieces=(), held_as=jnp.bfloat16):
    array = jax.random.normal(stream_key, extent, jnp.float32) * scale
    if len(pieces) > 0:
        array = block_scale(stream_key, extent, pieces, -0.22, 0.18) * array
    return jnp.clip(array, min=-bound, max=bound).astype(held_as)


def setup_inputs(seed: int = 0) -> dict:
    key_of = jax.random.split(jax.random.key(seed), 10)
    fields = scatter_about(key_of[0], (LAT_TOK, LONGITUDE_TOKENS, F * PATCH * PATCH), 1.0, 6.0, ((1, 8), (2, 16)))
    surf_weight = scatter_about(key_of[1], (NSURF, PATCH * PATCH, C), (PATCH * PATCH) ** -0.5, 0.625)
    atmos_weight = scatter_about(key_of[2], (NATM, PATCH * PATCH, C), (PATCH * PATCH) ** -0.5, 0.625)
    level_bias_table = scatter_about(key_of[3], (LEV, C), 1.0, 6.0, (), jnp.float32)
    latents = scatter_about(key_of[4], (LATENT, C), 1.0, 6.0)
    query_matrix = draw_query_matrix(jax.random.fold_in(key_of[9], 71), 0)
    key_weight = scatter_about(key_of[6], (C, C), C ** -0.5, 0.25)
    value_weight = scatter_about(key_of[7], (C, C), C ** -0.5, 0.25)
    out_weight = scatter_about(key_of[8], (C, C), C ** -0.5, 0.25)
    return dict(fields=fields, surf_weight=surf_weight, atmos_weight=atmos_weight, level_bias_table=level_bias_table, latents=latents, query_matrix=query_matrix, key_weight=key_weight, value_weight=value_weight, out_weight=out_weight)


def encode(block, surf_weight, atmos_weight, level_bias_table, latents, query_matrix, key_weight, value_weight, out_weight):
    tok_rows = block.shape[0]
    tok_cols = block.shape[1]
    count = tok_rows * tok_cols
    patch_tokens = block.reshape(count, F, PATCH * PATCH).astype(jnp.float32)
    surface = jnp.einsum('nfk,fkc->nc', patch_tokens[:, :NSURF], surf_weight.astype(jnp.float32))
    levels = jnp.zeros((count, LEV, C), jnp.float32) + level_bias_table
    for var in range(NATM):
        start = NSURF + var * LEV
        levels = levels + jnp.einsum('nlk,kc->nlc', patch_tokens[:, start:start + LEV], atmos_weight[var].astype(jnp.float32))
    centre = lax.optimization_barrier(jnp.mean(levels, axis=-1, keepdims=True))
    spread = lax.optimization_barrier(jnp.mean((levels - centre) ** 2, axis=-1, keepdims=True))
    normed = ((levels - centre) / jnp.sqrt(spread + 1e-05)).astype(jnp.bfloat16).astype(jnp.float32)
    key_vector = jnp.einsum('nlc,cd->nld', normed, key_weight.astype(jnp.float32)).astype(jnp.bfloat16)
    val_vec = jnp.einsum('nlc,cd->nld', normed, value_weight.astype(jnp.float32)).astype(jnp.bfloat16)
    key_vector = key_vector.astype(jnp.float32).reshape(count, LEV, HEADS, HEAD_CHANNELS)
    val_vec = val_vec.astype(jnp.float32).reshape(count, LEV, HEADS, HEAD_CHANNELS)
    query_rows = jnp.dot(latents, query_matrix, preferred_element_type=jnp.float32).astype(jnp.bfloat16)
    query_rows = query_rows.astype(jnp.float32).reshape(LATENT, HEADS, HEAD_CHANNELS)
    attention_logits = jnp.einsum('qix,nlix->iqln', query_rows, key_vector) / math.sqrt(HEAD_CHANNELS)
    attention_logits = attention_logits - lax.optimization_barrier(jnp.max(attention_logits, axis=2, keepdims=True))
    expo = jnp.exp(attention_logits)
    weights = (expo / lax.optimization_barrier(jnp.sum(expo, axis=2, keepdims=True))).astype(jnp.bfloat16).astype(jnp.float32)
    mixture = jnp.einsum('hmln,nlhd->nmhd', weights, val_vec).astype(jnp.bfloat16)
    mixture = mixture.astype(jnp.float32).reshape(count, LATENT, C)
    aggregated = latents.astype(jnp.float32) + jnp.einsum('nmc,cd->nmd', mixture, out_weight.astype(jnp.float32))
    joined = jnp.concatenate([surface[:, None, :], aggregated], axis=1).astype(jnp.bfloat16)
    return joined.reshape(tok_rows, tok_cols, LATENT + 1, C)

def reference(fields, surf_weight, atmos_weight, level_bias_table, latents, query_matrix, key_weight, value_weight, out_weight):

    def one_stripe(stripe):
        return encode(stripe[None], surf_weight, atmos_weight, level_bias_table, latents, query_matrix, key_weight, value_weight, out_weight)[0]
    return lax.map(one_stripe, fields)
```

```python
import functools
import math

import jax
import jax.numpy as jnp
from jax import lax
from jax.experimental import pallas as pl
from jax.experimental.pallas import tpu as pltpu
from jax.sharding import PartitionSpec as P

C = 512
HEADS = 16
HEAD_CHANNELS = 32
K = 100
NSURF = 4
NATM = 5
LATENT = 3
LEV = 12
NDEV = 16
FPD = 4
ROWS = 400
A = 8
COLS = 90
LANES = 128
BLK = 16
FULL = 5
REST = 10
REST_ROWS = 256
KT = 25
PAIRS = LEV // 2
QROWS = LATENT * HEADS

MESH = pl.DeviceIdType.MESH
BF16 = jnp.bfloat16
F32 = jnp.float32


def far_first():
    offsets = [(dy, dz, dc) for dy in range(4) for dz in range(2) for dc in range(2)][1:]
    return sorted(offsets, key=lambda o: -(min(o[0], 4 - o[0]) + o[1]))


OFFSETS = far_first()


def peer_of(me, offset):
    dy, dz, dc = offset
    y, z, c = me // 4, (me // 2) % 2, me % 2
    return ((y + dy) % 4) * 4 + ((z + dz) % 2) * 2 + (c + dc) % 2


def block_transpose(parts):
    lane = lax.broadcasted_iota(jnp.int32, parts[0].shape, 1)
    turned = [x if j == 0 else pltpu.roll(x, 8 * j, 1) for j, x in enumerate(parts)]
    held = [turned[-e % BLK] for e in range(BLK)]
    for s in (1, 2, 4, 8):
        mask = (lane & (8 * s)) != 0
        held = [jnp.where(mask, held[(e - s) % BLK], held[e]) for e in range(BLK)]
    return held


def kernel(
    fields_ref, surf_ref, atmos_ref, bias_ref, lat_ref, qm_ref, kw_ref, vw_ref, ow_ref,
    out_ref,
    inb, send, recv, unpacked, xs, wat, wvu, wsurf, biasb, vals, scores, mix, slots, outb,
    surf_v, atmos_v, bias_v, lat_v, qm_v, kw_v, vw_v, ow_v,
    in_sem, w_sem, send_sem, recv_sem, self_sem, out_sem,
):
    me = lax.axis_index("lat")

    loads = []
    for c in range(FULL + 1):
        n = BLK if c < FULL else REST
        loads.append(pltpu.make_async_copy(
            fields_ref.at[pl.ds(BLK * c, n)], inb.at[pl.ds(BLK * c, n)], in_sem.at[c]))
    loads[0].start()
    barrier = pltpu.get_barrier_semaphore()
    for o in OFFSETS:
        pl.semaphore_signal(barrier, inc=1, device_id={"lat": peer_of(me, o)}, device_id_type=MESH)
    for load in loads[1:]:
        load.start()
    weight_loads = []
    for i, (src, dst) in enumerate((
        (qm_ref, qm_v), (lat_ref, lat_v), (kw_ref, kw_v), (vw_ref, vw_v), (atmos_ref, atmos_v),
        (surf_ref, surf_v), (bias_ref, bias_v), (ow_ref, ow_v),
    )):
        weight_loads.append(pltpu.make_async_copy(src, dst, w_sem.at[i]))
        weight_loads[-1].start()

    def shuffle_full(c):
        def tile(t, carry):
            rows = pl.ds(pl.multiple_of(16 * t, 16), 16)
            parts = [inb[BLK * c + j, rows, :] for j in range(BLK)]
            for e, y in enumerate(block_transpose(parts)):
                send[c, e, rows, :] = y
            return carry
        lax.fori_loop(0, KT, tile, 0)

    def shuffle_rest():
        def group(g, carry):
            parts = []
            for j in range(BLK):
                n = lax.rem(BLK * g + j, KT * REST)
                t = n // REST
                parts.append(inb[BLK * FULL + n - t * REST, pl.ds(pl.multiple_of(16 * t, 16), 16), :])
            rows = pl.ds(pl.multiple_of(16 * g, 16), 16)
            for e, y in enumerate(block_transpose(parts)):
                send[FULL, e, rows, :] = y if e == 0 else pltpu.roll(y, LANES - 8 * e, 1)
            return carry
        lax.fori_loop(0, BLK, group, 0)

    def own(c):
        rows = pl.ds(0, ROWS if c < FULL else REST_ROWS)
        return pltpu.make_async_copy(send.at[c, me, rows], recv.at[c, me, rows], self_sem.at[c])

    def ship(c):
        rows = pl.ds(0, ROWS if c < FULL else REST_ROWS)
        for o in OFFSETS:
            d = peer_of(me, o)
            pltpu.make_async_remote_copy(
                src_ref=send.at[c, d, rows], dst_ref=recv.at[c, me, rows],
                send_sem=send_sem.at[c], recv_sem=recv_sem.at[c],
                device_id={"lat": d}, device_id_type=MESH,
            ).start()
        own(c).start()

    for c in range(FULL + 1):
        loads[c].wait()
        if c < FULL:
            shuffle_full(c)
        else:
            shuffle_rest()
        if c == 0:
            pl.semaphore_wait(barrier, NDEV - 1)
        ship(c)

    for load in weight_loads:
        load.wait()
    queries = jnp.dot(lat_v[...], qm_v[...], preferred_element_type=F32).astype(BF16).astype(F32)
    channel_head = lax.broadcasted_iota(jnp.int32, (HEADS, C), 1) // HEAD_CHANNELS
    own_head = channel_head == lax.broadcasted_iota(jnp.int32, (HEADS, C), 0)
    spread = jnp.concatenate(
        [jnp.where(own_head, jnp.broadcast_to(queries[m : m + 1], (HEADS, C)), 0.0) for m in range(LATENT)],
        axis=0,
    ).astype(BF16)
    score_w = lax.dot_general(
        spread, kw_v[...], (((1,), (1,)), ((), ())), preferred_element_type=F32
    ) * (1.0 / math.sqrt(HEAD_CHANNELS))
    high = score_w.astype(BF16)
    wvu[pl.ds(0, C), :] = vw_v[...].astype(F32).T.astype(BF16)
    wvu[pl.ds(C, QROWS), :] = high
    wvu[pl.ds(C + QROWS, QROWS), :] = (score_w - high.astype(F32)).astype(BF16)
    stacked = jnp.concatenate(
        [atmos_v[v].astype(F32) for v in range(NATM)] + [jnp.zeros((C - NATM * K, C), F32)], axis=0
    )
    wat[...] = stacked.T.astype(BF16)
    wsurf[...] = jnp.concatenate([surf_v[f].astype(F32) for f in range(NSURF)], axis=0).astype(BF16)

    def spread_bias(l, carry):
        row = bias_v[pl.ds(l, 1), :]
        biasb[l] = jnp.broadcast_to(row, (LANES, C)).T
        return carry
    lax.fori_loop(0, LEV, spread_bias, 0)
    xs[:, pl.ds(C - 16, 16), :] = jnp.zeros((PAIRS, 16, 2 * LANES), BF16)

    def unpack(s, carry):
        lane = lax.broadcasted_iota(jnp.int32, (16, LANES), 1)
        for t in range(KT):
            g, off = divmod(8 * REST * t, LANES)
            x = recv[FULL, s, 16 * g : 16 * g + 16, :]
            if off:
                x = pltpu.roll(x, LANES - off, 1)
            if off + 8 * REST > LANES:
                y = pltpu.roll(recv[FULL, s, 16 * g + 16 : 16 * g + 32, :], LANES - off, 1)
                x = jnp.where(lane < LANES - off, x, y)
            unpacked[s, 16 * t : 16 * t + 16, :] = x
        return carry

    def out_copy(c, slot):
        n = BLK if c < FULL else REST
        return pltpu.make_async_copy(
            outb.at[slot, :, pl.ds(0, n)], out_ref.at[:, pl.ds(BLK * c, n)], out_sem.at[slot])

    def process(block, turn, slot):
        for s in range(1, NDEV):
            v, g = divmod(s - 1, 3)
            for j in range(FPD):
                l = 4 * g + j
                xs[l // 2, pl.ds(K * v, K), pl.ds((l % 2) * LANES, LANES)] = block[s, pl.ds(K * j, K), :]

        def pair(p, carry):
            levels = jnp.dot(wat[...], xs[p], preferred_element_type=F32)
            levels = levels + jnp.concatenate([biasb[2 * p], biasb[2 * p + 1]], axis=1)
            centred = levels - jnp.sum(levels, axis=0, keepdims=True) * (1.0 / C)
            var = jnp.sum(centred * centred, axis=0, keepdims=True) * (1.0 / C)
            normed = (centred * lax.rsqrt(var + 1e-5)).astype(BF16)
            got = jnp.dot(wvu[...], normed, preferred_element_type=F32)
            for i in range(2):
                half = got[:, i * LANES : (i + 1) * LANES]
                vals[2 * p + i] = half[:C].astype(BF16)
                scores[2 * p + i] = half[C : C + QROWS] + half[C + QROWS :]
            return carry
        lax.fori_loop(0, PAIRS, pair, 0)

        top = scores[0]
        for l in range(1, LEV):
            top = jnp.maximum(top, scores[l])
        total = jnp.zeros((QROWS, LANES), F32)
        for l in range(LEV):
            e = jnp.exp(scores[l] - top)
            scores[l] = e
            total = total + e
        for l in range(LEV):
            scores[l] = (scores[l] / total).astype(BF16).astype(F32)

        def head(h, carry):
            rows = pl.ds(pl.multiple_of(HEAD_CHANNELS * h, HEAD_CHANNELS), HEAD_CHANNELS)
            sums = [jnp.zeros((HEAD_CHANNELS, LANES), F32) for _ in range(LATENT)]
            for l in range(LEV):
                val = vals[l, rows, :].astype(F32)
                for m in range(LATENT):
                    sums[m] = sums[m] + scores[l, pl.ds(m * HEADS + h, 1), :] * val
            for m in range(LATENT):
                mix[m, rows, :] = sums[m].astype(BF16)
            return carry
        lax.fori_loop(0, HEADS, head, 0)

        surf = lax.dot_general(block[0], wsurf[...], (((0,), (0,)), ((), ())), preferred_element_type=F32)
        slots[:, 0, :] = surf
        for m in range(LATENT):
            agg = lax.dot_general(mix[m], ow_v[...], (((0,), (0,)), ((), ())), preferred_element_type=F32)
            slots[:, m + 1, :] = agg + lat_v[pl.ds(m, 1), :].astype(F32)

        def place(j, carry):
            start = pl.multiple_of(A * lax.rem(j + turn, BLK), A)
            for a in range(A):
                outb[slot, a, j] = slots[start + a].astype(BF16)
            return carry
        lax.fori_loop(0, BLK, place, 0)

    def wait_recv(c):
        rows = pl.ds(0, ROWS if c < FULL else REST_ROWS)
        whole = recv.at[c, pl.ds(0, NDEV - 1), rows]
        pltpu.make_async_copy(whole, whole, recv_sem.at[c]).wait()
        own(c).wait()

    for c in range(FULL + 1):
        slot = c % 2
        wait_recv(c)
        if c >= 2:
            out_copy(c - 2, slot).wait()
        if c < FULL:
            process(recv.at[c], me, slot)
        else:
            lax.fori_loop(0, NDEV, unpack, 0)
            process(unpacked, 0, slot)
        out_copy(c, slot).start()
    out_copy(FULL - 1, (FULL - 1) % 2).wait()
    out_copy(FULL, FULL % 2).wait()
    for c in range(FULL + 1):
        rows = pl.ds(0, ROWS if c < FULL else REST_ROWS)
        whole = send.at[c, pl.ds(0, NDEV - 1), rows]
        pltpu.make_async_copy(whole, whole, send_sem.at[c]).wait()


def shards(fields, surf_weight, atmos_weight, level_bias_table, latents, query_matrix, key_weight, value_weight, out_weight):
    by_token = jnp.transpose(fields, (1, 2, 0))
    any_spec = pl.BlockSpec(memory_space=pl.ANY)
    dma = pltpu.SemaphoreType.DMA
    return pl.pallas_call(
        kernel,
        out_shape=jax.ShapeDtypeStruct((A, COLS, LATENT + 1, C), BF16),
        in_specs=[any_spec] * 9,
        out_specs=any_spec,
        scratch_shapes=[
            pltpu.VMEM((COLS, ROWS, LANES), BF16),
            pltpu.VMEM((FULL + 1, NDEV, ROWS, LANES), BF16),
            pltpu.VMEM((FULL + 1, NDEV, ROWS, LANES), BF16),
            pltpu.VMEM((NDEV, ROWS, LANES), BF16),
            pltpu.VMEM((PAIRS, C, 2 * LANES), BF16),
            pltpu.VMEM((C, C), BF16),
            pltpu.VMEM((C + 2 * QROWS, C), BF16),
            pltpu.VMEM((NSURF * K, C), BF16),
            pltpu.VMEM((LEV, C, LANES), F32),
            pltpu.VMEM((LEV, C, LANES), BF16),
            pltpu.VMEM((LEV, QROWS, LANES), F32),
            pltpu.VMEM((LATENT, C, LANES), BF16),
            pltpu.VMEM((LANES, LATENT + 1, C), F32),
            pltpu.VMEM((2, A, BLK, LATENT + 1, C), BF16),
            pltpu.VMEM(surf_weight.shape, BF16),
            pltpu.VMEM(atmos_weight.shape, BF16),
            pltpu.VMEM(level_bias_table.shape, F32),
            pltpu.VMEM(latents.shape, BF16),
            pltpu.VMEM(query_matrix.shape, BF16),
            pltpu.VMEM(key_weight.shape, BF16),
            pltpu.VMEM(value_weight.shape, BF16),
            pltpu.VMEM(out_weight.shape, BF16),
            dma((FULL + 1,)),
            dma((8,)),
            dma((FULL + 1,)),
            dma((FULL + 1,)),
            dma((FULL + 1,)),
            dma((2,)),
        ],
        compiler_params=pltpu.CompilerParams(
            collective_id=0, has_side_effects=True, vmem_limit_bytes=60 * 2**20
        ),
        name="exchange_and_encode",
    )(by_token, surf_weight, atmos_weight, level_bias_table, latents, query_matrix, key_weight, value_weight, out_weight)


def solution(mesh):
    in_specs = (P(None, "lon", "lat"), P(), P(), P(), P(), P(), P(), P(), P())
    out_specs = P("lat", "lon", None, None)
    return jax.shard_map(shards, mesh=mesh, in_specs=in_specs, out_specs=out_specs, check_vma=False)
```

```python
import functools
import math

import jax
import jax.numpy as jnp
from jax import lax
from jax.experimental import pallas as pl
from jax.experimental.pallas import tpu as pltpu
from jax.sharding import PartitionSpec as P

C = 512
HEADS = 16
HEAD_CHANNELS = 32
K = 100
NSURF = 4
NATM = 5
LATENT = 3
LEV = 12
NDEV = 16
FPD = 4
ROWS = 400
A = 8
COLS = 90
LANES = 128
BLK = 16
FULL = 5
REST = 10
REST_ROWS = 256
KT = 25
QROWS = LATENT * HEADS
LAST = FULL - 1
PIECES = ((0, 208), (208, 304), (304, 400))
EARLY = 5 * BLK

MESH = pl.DeviceIdType.MESH
BF16 = jnp.bfloat16
F32 = jnp.float32


def far_first():
    offsets = [(dy, dz, dc) for dy in range(4) for dz in range(2) for dc in range(2)][1:]
    return sorted(offsets, key=lambda o: -(min(o[0], 4 - o[0]) + o[1]))


OFFSETS = far_first()


def peer_of(me, offset):
    dy, dz, dc = offset
    y, z, c = me // 4, (me // 2) % 2, me % 2
    return ((y + dy) % 4) * 4 + ((z + dz) % 2) * 2 + (c + dc) % 2


def block_transpose(parts):
    lane = lax.broadcasted_iota(jnp.int32, parts[0].shape, 1)
    turned = [x if j == 0 else pltpu.roll(x, 8 * j, 1) for j, x in enumerate(parts)]
    held = [turned[-e % BLK] for e in range(BLK)]
    for s in (1, 2, 4, 8):
        mask = (lane & (8 * s)) != 0
        held = [jnp.where(mask, held[(e - s) % BLK], held[e]) for e in range(BLK)]
    return held


def project(block, mix, wsurf, ow, lat, slots):
    contract = (((0,), (0,)), ((), ()))
    slots[:, 0, :] = lax.dot_general(block[...], wsurf[...], contract, preferred_element_type=F32)
    for m in range(LATENT):
        agg = lax.dot_general(mix[m], ow[...], contract, preferred_element_type=F32)
        slots[:, m + 1, :] = agg + lat[pl.ds(m, 1), :].astype(F32)


def kernel(
    fields_ref, surf_ref, atmos_ref, bias_ref, lat_ref, qm_ref, kw_ref, vw_ref, ow_ref,
    staged, mix, last_surf, wsurf, ow_v, lat_v,
    inb, send, recv, xs, wat, wvu, biasb, vals, scores, slots,
    surf_v, atmos_v, bias_v, qm_v, kw_v, vw_v,
    in_sem, w_sem, send_sem, recv_sem, piece_sem, self_sem,
):
    me = lax.axis_index("lat")
    rest_raw, rest_done = FULL, FULL + 1

    def load(c, n=BLK):
        here = pl.ds(BLK * c, n)
        return pltpu.make_async_copy(fields_ref.at[here], inb.at[here], in_sem.at[c])

    load(0).start()
    barrier = pltpu.get_barrier_semaphore()
    for o in OFFSETS:
        pl.semaphore_signal(barrier, inc=1, device_id={"lat": peer_of(me, o)}, device_id_type=MESH)
    for c in range(1, FULL):
        load(c).start()
    load(FULL, REST).start()
    weight_loads = []
    for i, (src, dst) in enumerate((
        (qm_ref, qm_v), (lat_ref, lat_v), (kw_ref, kw_v), (vw_ref, vw_v), (atmos_ref, atmos_v),
        (surf_ref, surf_v), (bias_ref, bias_v), (ow_ref, ow_v),
    )):
        weight_loads.append(pltpu.make_async_copy(src, dst, w_sem.at[i]))
        weight_loads[-1].start()

    def unturn(e, y):
        return y if e == 0 else pltpu.roll(y, LANES - 8 * e, 1)

    def shuffle_full(c, straight=False):
        def tile(t, carry):
            rows = pl.ds(pl.multiple_of(16 * t, 16), 16)
            parts = [inb[BLK * c + j, rows, :] for j in range(BLK)]
            for e, y in enumerate(block_transpose(parts)):
                send[c, e, rows, :] = unturn(e, y) if straight else y
            return carry
        lax.fori_loop(0, KT, tile, 0, unroll=5)

    def rest_group(q, g, count):
        parts = []
        for j in range(BLK):
            t, b = divmod(BLK * g + j, REST) if j < count else (0, j - count)
            rows = pl.ds(pl.multiple_of(128 * q + 16 * t, 16), 16)
            parts.append(inb[BLK * FULL + b, rows, :])
        rows = pl.ds(pl.multiple_of(80 * q + 16 * g, 16), 16)
        for e, y in enumerate(block_transpose(parts)):
            send[FULL, e, rows, :] = unturn(e, y)

    def shuffle_rest():
        def five(q, carry):
            for g in range(5):
                rest_group(q, g, BLK)
            return carry
        lax.fori_loop(0, 3, five, 0)
        rest_group(3, 0, REST)

    def own(c, start, stop, sem):
        rows = pl.ds(start, stop - start)
        return pltpu.make_async_copy(send.at[c, me, rows], recv.at[c, me, rows], sem)

    def ship(c, start, stop, sem, own_sem):
        rows = pl.ds(start, stop - start)
        for o in OFFSETS:
            d = peer_of(me, o)
            pltpu.make_async_remote_copy(
                src_ref=send.at[c, d, rows], dst_ref=recv.at[c, me, rows],
                send_sem=send_sem.at[c], recv_sem=sem,
                device_id={"lat": d}, device_id_type=MESH,
            ).start()
        own(c, start, stop, own_sem).start()

    def ship_whole(c, rows):
        ship(c, 0, rows, recv_sem.at[c], self_sem.at[c])

    load(0).wait()
    shuffle_full(0)
    pl.semaphore_wait(barrier, NDEV - 1)
    ship_whole(0, ROWS)

    def send_next(c, carry):
        load(c).wait()
        shuffle_full(c)
        ship_whole(c, ROWS)
        return carry
    lax.fori_loop(1, LAST, send_next, 0)
    load(FULL, REST).wait()
    shuffle_rest()
    ship_whole(FULL, REST_ROWS)
    load(LAST).wait()
    shuffle_full(LAST, straight=True)
    for i, (start, stop) in enumerate(PIECES):
        ship(LAST, start, stop, piece_sem.at[i], self_sem.at[FULL + 1 + i])

    for w in weight_loads:
        w.wait()
    queries = jnp.dot(lat_v[...], qm_v[...], preferred_element_type=F32).astype(BF16).astype(F32)
    channel_head = lax.broadcasted_iota(jnp.int32, (HEADS, C), 1) // HEAD_CHANNELS
    own_head = channel_head == lax.broadcasted_iota(jnp.int32, (HEADS, C), 0)
    spread = jnp.concatenate(
        [jnp.where(own_head, jnp.broadcast_to(queries[m : m + 1], (HEADS, C)), 0.0) for m in range(LATENT)],
        axis=0,
    ).astype(BF16)
    score_w = lax.dot_general(
        spread, kw_v[...], (((1,), (1,)), ((), ())), preferred_element_type=F32
    ) * (1.0 / math.sqrt(HEAD_CHANNELS))
    high = score_w.astype(BF16)
    wvu[pl.ds(0, C), :] = vw_v[...].astype(F32).T.astype(BF16)
    wvu[pl.ds(C, QROWS), :] = high
    wvu[pl.ds(C + QROWS, QROWS), :] = (score_w - high.astype(F32)).astype(BF16)
    stacked = jnp.concatenate(
        [atmos_v[v].astype(F32) for v in range(NATM)] + [jnp.zeros((C - NATM * K, C), F32)], axis=0
    )
    wat[...] = stacked.T.astype(BF16)
    wsurf[...] = jnp.concatenate([surf_v[:, f, :].astype(F32) for f in range(NSURF)], axis=0).astype(BF16)

    for n in range(LEV):
        l = 4 * (n % 3) + n // 3
        biasb[n] = jnp.broadcast_to(bias_v[pl.ds(l, 1), :], (LANES, C)).T
    xs[pl.ds(C - 16, 16), :] = jnp.zeros((16, LEV * LANES), BF16)

    def unpack(s, carry):
        lane = lax.broadcasted_iota(jnp.int32, (16, LANES), 1)
        for t in range(KT):
            g, off = divmod(8 * REST * t, LANES)
            x = recv[rest_raw, s, 16 * g : 16 * g + 16, :]
            if off:
                x = pltpu.roll(x, LANES - off, 1)
            if off + 8 * REST > LANES:
                y = pltpu.roll(recv[rest_raw, s, 16 * g + 16 : 16 * g + 32, :], LANES - off, 1)
                x = jnp.where(lane < LANES - off, x, y)
            recv[rest_done, s, 16 * t : 16 * t + 16, :] = x
        return carry

    def gather(place, j):
        for s in range(1, NDEV):
            v, g = divmod(s - 1, 3)
            xs[pl.ds(K * v, K), pl.ds((3 * j + g) * LANES, LANES)] = recv[place, s, pl.ds(K * j, K), :]

    def embed(first, count):
        cols = pl.ds(first * LANES, count * LANES)
        levels = jnp.dot(wat[...], xs[:, cols], preferred_element_type=F32)
        levels = levels + jnp.concatenate([biasb[first + i] for i in range(count)], axis=1)
        centred = levels - jnp.sum(levels, axis=0, keepdims=True) * (1.0 / C)
        var = jnp.sum(centred * centred, axis=0, keepdims=True) * (1.0 / C)
        xs[:, cols] = (centred * lax.rsqrt(var + 1e-5)).astype(BF16)

    def attend(first, count):
        got = jnp.dot(wvu[...], xs[:, pl.ds(first * LANES, count * LANES)], preferred_element_type=F32)
        for i in range(count):
            part = got[:, i * LANES : (i + 1) * LANES]
            vals[first + i] = part[:C].astype(BF16)
            scores[first + i] = part[C : C + QROWS] + part[C + QROWS :]

    def softmax():
        top = scores[0]
        for l in range(1, LEV):
            top = jnp.maximum(top, scores[l])
        total = jnp.zeros((QROWS, LANES), F32)
        for l in range(LEV):
            e = jnp.exp(scores[l] - top)
            scores[l] = e
            total = total + e
        for l in range(LEV):
            scores[l] = (scores[l] / total).astype(BF16).astype(F32)

    def mixture():
        def head(h, carry):
            rows = pl.ds(pl.multiple_of(HEAD_CHANNELS * h, HEAD_CHANNELS), HEAD_CHANNELS)
            sums = [jnp.zeros((HEAD_CHANNELS, LANES), F32) for _ in range(LATENT)]
            for l in range(LEV):
                val = vals[l, rows, :].astype(F32)
                for m in range(LATENT):
                    sums[m] = sums[m] + scores[l, pl.ds(m * HEADS + h, 1), :] * val
            for m in range(LATENT):
                mix[m, rows, :] = sums[m].astype(BF16)
            return carry
        lax.fori_loop(0, HEADS, head, 0)

    def lay_out(t, turn):
        def move(j, carry):
            start = pl.multiple_of(A * lax.rem(j + turn, BLK), A)
            for a in range(A):
                staged[a, BLK * t + j] = slots[start + a].astype(BF16)
            return carry
        lax.fori_loop(0, BLK, move, 0, unroll=2)

    def arrived(c, start, stop, sem, own_sem):
        whole = recv.at[c, pl.ds(0, NDEV - 1), pl.ds(start, stop - start)]
        pltpu.make_async_copy(whole, whole, sem).wait()
        own(c, start, stop, own_sem).wait()

    def process(t, carry):
        is_rest = t // LAST
        place = t + is_rest * (rest_done - LAST)

        @pl.when(t < LAST)
        def _():
            arrived(t, 0, ROWS, recv_sem.at[t], self_sem.at[t])

        @pl.when(t == LAST)
        def _():
            arrived(FULL, 0, REST_ROWS, recv_sem.at[FULL], self_sem.at[FULL])
            lax.fori_loop(0, NDEV, unpack, 0, unroll=2)

        for j in range(FPD):
            gather(place, j)
        for p in range(LEV // 2):
            embed(2 * p, 2)
        for p in range(LEV // 2):
            attend(2 * p, 2)
        softmax()
        mixture()
        project(recv.at[place, 0], mix, wsurf, ow_v, lat_v, slots)
        lay_out(t, me * (1 - is_rest))
        return carry
    lax.fori_loop(0, FULL, process, 0)

    done = 0
    for i, (start, stop) in enumerate(PIECES):
        arrived(LAST, start, stop, piece_sem.at[i], self_sem.at[FULL + 1 + i])
        while done < FPD and K * (done + 1) <= stop:
            gather(LAST, done)
            done += 1
        if i == 0:
            groups = ((0, 2), (2, 2), (4, 2))
        else:
            groups = ((3 * (done - 1), 3),)
        for group in groups:
            embed(*group)
        for group in groups:
            attend(*group)
        rows = pl.ds(start, stop - start)
        last_surf[rows, :] = recv[LAST, 0, rows, :]
    softmax()
    mixture()

    for c in range(FULL + 1):
        whole = send.at[c, pl.ds(0, NDEV - 1), pl.ds(0, ROWS if c < FULL else REST_ROWS)]
        pltpu.make_async_copy(whole, whole, send_sem.at[c]).wait()


def finish(staged, mix, last_surf, wsurf, ow, lat, out_ref, slots, outb, sem):
    ahead = BLK * LAST
    writes = [
        pltpu.make_async_copy(staged.at[:, pl.ds(0, ahead)], out_ref.at[:, pl.ds(0, ahead)], sem.at[0]),
        pltpu.make_async_copy(staged.at[:, pl.ds(ahead, REST)], out_ref.at[:, pl.ds(BLK * FULL, REST)], sem.at[1]),
    ]
    for write in writes:
        write.start()
    project(last_surf, mix, wsurf, ow, lat, slots)

    def move(j, carry):
        start = pl.multiple_of(A * j, A)
        for a in range(A):
            outb[a, j] = slots[start + a].astype(BF16)
        return carry
    lax.fori_loop(0, BLK, move, 0, unroll=2)
    writes.append(pltpu.make_async_copy(outb, out_ref.at[:, pl.ds(ahead, BLK)], sem.at[2]))
    writes[-1].start()
    for write in writes:
        write.wait()


def shards(fields, surf_weight, atmos_weight, level_bias_table, latents, query_matrix, key_weight, value_weight, out_weight):
    by_token = jnp.transpose(fields, (1, 2, 0))
    surf_cells = jnp.transpose(surf_weight, (1, 0, 2))
    operands = (
        by_token, surf_cells, atmos_weight, level_bias_table, latents,
        query_matrix, key_weight, value_weight, out_weight,
    )
    in_hbm = pl.BlockSpec(memory_space=pl.ANY)
    in_vmem = pl.BlockSpec(memory_space=pltpu.VMEM)
    dma = pltpu.SemaphoreType.DMA
    handed = pl.pallas_call(
        kernel,
        out_shape=[
            pltpu.VMEM((A, EARLY, LATENT + 1, C), BF16),
            pltpu.VMEM((LATENT, C, LANES), BF16),
            pltpu.VMEM((ROWS, LANES), BF16),
            pltpu.VMEM((NSURF * K, C), BF16),
            pltpu.VMEM((C, C), BF16),
            pltpu.VMEM((LATENT, C), BF16),
        ],
        in_specs=[in_hbm] * 9,
        out_specs=[in_vmem] * 6,
        scratch_shapes=[
            pltpu.VMEM((COLS, ROWS, LANES), BF16),
            pltpu.VMEM((FULL + 1, NDEV, ROWS, LANES), BF16),
            pltpu.VMEM((FULL + 2, NDEV, ROWS, LANES), BF16),
            pltpu.VMEM((C, LEV * LANES), BF16),
            pltpu.VMEM((C, C), BF16),
            pltpu.VMEM((C + 2 * QROWS, C), BF16),
            pltpu.VMEM((LEV, C, LANES), F32),
            pltpu.VMEM((LEV, C, LANES), BF16),
            pltpu.VMEM((LEV, QROWS, LANES), F32),
            pltpu.VMEM((LANES, LATENT + 1, C), F32),
            pltpu.VMEM(surf_cells.shape, BF16),
            pltpu.VMEM(atmos_weight.shape, BF16),
            pltpu.VMEM(level_bias_table.shape, F32),
            pltpu.VMEM(query_matrix.shape, BF16),
            pltpu.VMEM(key_weight.shape, BF16),
            pltpu.VMEM(value_weight.shape, BF16),
            dma((FULL + 1,)),
            dma((8,)),
            dma((FULL + 1,)),
            dma((FULL + 1,)),
            dma((len(PIECES),)),
            dma((FULL + 1 + len(PIECES),)),
        ],
        compiler_params=pltpu.CompilerParams(
            collective_id=0, has_side_effects=True, vmem_limit_bytes=48 * 2**20
        ),
        name="exchange_and_encode",
    )(*[pltpu.with_memory_space_constraint(x, pltpu.HBM) for x in operands])
    return pl.pallas_call(
        finish,
        out_shape=jax.ShapeDtypeStruct((A, COLS, LATENT + 1, C), BF16),
        in_specs=[in_vmem] * 6,
        out_specs=in_hbm,
        scratch_shapes=[
            pltpu.VMEM((LANES, LATENT + 1, C), F32),
            pltpu.VMEM((A, BLK, LATENT + 1, C), BF16),
            dma((3,)),
        ],
        compiler_params=pltpu.CompilerParams(vmem_limit_bytes=8 * 2**20),
        name="finish",
    )(*[pltpu.with_memory_space_constraint(x, pltpu.VMEM) for x in handed])


def solution(mesh):
    in_specs = (P(None, "lon", "lat"), P(), P(), P(), P(), P(), P(), P(), P())
    out_specs = P("lat", "lon", None, None)
    return jax.shard_map(shards, mesh=mesh, in_specs=in_specs, out_specs=out_specs, check_vma=False)
```

```python
import functools
import math

import jax
import jax.numpy as jnp
from jax import lax
from jax.experimental import pallas as pl
from jax.experimental.pallas import tpu as pltpu
from jax.sharding import PartitionSpec as P

C = 512
HEADS = 16
HEAD_CHANNELS = 32
K = 100
NSURF = 4
NATM = 5
LATENT = 3
LEV = 12
NDEV = 16
FPD = 4
ROWS = 400
A = 8
COLS = 90
LANES = 128
BLK = 16
FULL = 5
REST = 10
REST_ROWS = 256
KT = 25
QROWS = LATENT * HEADS
LAST = FULL - 1
OPENING = 80
PIECES = ((0, 208), (208, 304), (304, 400))
EARLY = 5 * BLK

MESH = pl.DeviceIdType.MESH
BF16 = jnp.bfloat16
F32 = jnp.float32


def far_first():
    offsets = [(dy, dz, dc) for dy in range(4) for dz in range(2) for dc in range(2)][1:]
    return sorted(offsets, key=lambda o: -(min(o[0], 4 - o[0]) + o[1]))


OFFSETS = far_first()


def peer_of(me, offset):
    dy, dz, dc = offset
    y, z, c = me // 4, (me // 2) % 2, me % 2
    return ((y + dy) % 4) * 4 + ((z + dz) % 2) * 2 + (c + dc) % 2


def block_transpose(parts):
    lane = lax.broadcasted_iota(jnp.int32, parts[0].shape, 1)
    turned = [x if j == 0 else pltpu.roll(x, 8 * j, 1) for j, x in enumerate(parts)]
    held = [turned[-e % BLK] for e in range(BLK)]
    for s in (1, 2, 4, 8):
        mask = (lane & (8 * s)) != 0
        held = [jnp.where(mask, held[(e - s) % BLK], held[e]) for e in range(BLK)]
    return held


def mixture(terms, shares, out):
    for h in range(HEADS):
        rows = pl.ds(HEAD_CHANNELS * h, HEAD_CHANNELS)
        sums = [None] * LATENT
        for i, values in terms:
            held = [values(m)[rows, :] for m in range(LATENT)] if callable(values) else [values[rows, :]] * LATENT
            for m in range(LATENT):
                term = shares[i, pl.ds(m * HEADS + h, 1), :] * held[m]
                sums[m] = term if sums[m] is None else sums[m] + term
        for m in range(LATENT):
            out[m, rows, :] = sums[m].astype(out.dtype)


def project(block, mix, wsurf, ow, lat, slots):
    contract = (((0,), (0,)), ((), ()))
    slots[:, 0, :] = lax.dot_general(block[...], wsurf[...], contract, preferred_element_type=F32)
    for m in range(LATENT):
        agg = lax.dot_general(mix[m], ow[...], contract, preferred_element_type=F32)
        slots[:, m + 1, :] = agg + lat[pl.ds(m, 1), :].astype(F32)


def kernel(
    fields_ref, surf_ref, atmos_ref, bias_ref, lat_ref, qm_ref, kw_ref, vw_ref, ow_ref,
    staged, mix, last_surf, wsurf, ow_v, lat_v,
    inb, send, recv, xs, wat, wuv, biasb, vals, scores, part, slots,
    surf_v, atmos_v, bias_v, qm_v, kw_v, vw_v,
    in_sem, w_sem, send_sem, recv_sem, piece_sem, self_sem,
):
    me = lax.axis_index("lat")
    rest_raw, rest_done = FULL, FULL + 1

    def load(c, n=BLK, start=0, stop=ROWS, sem=None):
        here, rows = pl.ds(BLK * c, n), pl.ds(start, stop - start)
        return pltpu.make_async_copy(
            fields_ref.at[here, rows], inb.at[here, rows], in_sem.at[c if sem is None else sem])

    load(0, stop=OPENING).start()
    barrier = pltpu.get_barrier_semaphore()
    for o in OFFSETS:
        pl.semaphore_signal(barrier, inc=1, device_id={"lat": peer_of(me, o)}, device_id_type=MESH)
    load(0, start=OPENING, sem=FULL + 1).start()
    for c in range(1, FULL):
        load(c).start()
    load(FULL, REST).start()
    weight_loads = []
    for i, (src, dst) in enumerate((
        (qm_ref, qm_v), (lat_ref, lat_v), (kw_ref, kw_v), (vw_ref, vw_v), (atmos_ref, atmos_v),
        (surf_ref, surf_v), (bias_ref, bias_v), (ow_ref, ow_v),
    )):
        weight_loads.append(pltpu.make_async_copy(src, dst, w_sem.at[i]))
        weight_loads[-1].start()

    def unturn(e, y):
        return y if e == 0 else pltpu.roll(y, LANES - 8 * e, 1)

    def shuffle_full(c, straight=False, start=0, stop=ROWS):
        def tile(t, carry):
            rows = pl.ds(pl.multiple_of(16 * t, 16), 16)
            parts = [inb[BLK * c + j, rows, :] for j in range(BLK)]
            for e, y in enumerate(block_transpose(parts)):
                send[c, e, rows, :] = unturn(e, y) if straight else y
            return carry
        lax.fori_loop(start // 16, stop // 16, tile, 0, unroll=5)

    def rest_group(q, g, count):
        parts = []
        for j in range(BLK):
            t, b = divmod(BLK * g + j, REST) if j < count else (0, j - count)
            rows = pl.ds(pl.multiple_of(128 * q + 16 * t, 16), 16)
            parts.append(inb[BLK * FULL + b, rows, :])
        rows = pl.ds(pl.multiple_of(80 * q + 16 * g, 16), 16)
        for e, y in enumerate(block_transpose(parts)):
            send[FULL, e, rows, :] = unturn(e, y)

    def shuffle_rest():
        def five(q, carry):
            for g in range(5):
                rest_group(q, g, BLK)
            return carry
        lax.fori_loop(0, 3, five, 0)
        rest_group(3, 0, REST)

    def own(c, start, stop, sem):
        rows = pl.ds(start, stop - start)
        return pltpu.make_async_copy(send.at[c, me, rows], recv.at[c, me, rows], sem)

    def ship(c, start, stop, sem, own_sem):
        rows = pl.ds(start, stop - start)
        for o in OFFSETS:
            d = peer_of(me, o)
            pltpu.make_async_remote_copy(
                src_ref=send.at[c, d, rows], dst_ref=recv.at[c, me, rows],
                send_sem=send_sem.at[c], recv_sem=sem,
                device_id={"lat": d}, device_id_type=MESH,
            ).start()
        own(c, start, stop, own_sem).start()

    def ship_whole(c, rows):
        ship(c, 0, rows, recv_sem.at[c], self_sem.at[c])

    load(0, stop=OPENING).wait()
    shuffle_full(0, stop=OPENING)
    pl.semaphore_wait(barrier, NDEV - 1)
    ship(0, 0, OPENING, recv_sem.at[0], self_sem.at[0])
    load(0, start=OPENING, sem=FULL + 1).wait()
    shuffle_full(0, start=OPENING)
    ship(0, OPENING, ROWS, recv_sem.at[0], self_sem.at[0])

    def send_next(c, carry):
        load(c).wait()
        shuffle_full(c)
        ship_whole(c, ROWS)
        return carry
    lax.fori_loop(1, LAST, send_next, 0)
    load(FULL, REST).wait()
    shuffle_rest()
    ship_whole(FULL, REST_ROWS)
    load(LAST).wait()
    shuffle_full(LAST, straight=True)
    for i, (start, stop) in enumerate(PIECES):
        ship(LAST, start, stop, piece_sem.at[i], self_sem.at[FULL + 1 + i])

    for w in weight_loads:
        w.wait()
    queries = jnp.dot(lat_v[...], qm_v[...], preferred_element_type=F32).astype(BF16).astype(F32)
    channel_head = lax.broadcasted_iota(jnp.int32, (HEADS, C), 1) // HEAD_CHANNELS
    own_head = channel_head == lax.broadcasted_iota(jnp.int32, (HEADS, C), 0)
    spread = jnp.concatenate(
        [jnp.where(own_head, jnp.broadcast_to(queries[m : m + 1], (HEADS, C)), 0.0) for m in range(LATENT)],
        axis=0,
    ).astype(BF16)
    score_w = lax.dot_general(
        spread, kw_v[...], (((1,), (1,)), ((), ())), preferred_element_type=F32
    ) * (1.0 / math.sqrt(HEAD_CHANNELS))
    high = score_w.astype(BF16)
    wuv[pl.ds(0, QROWS), :] = high
    wuv[pl.ds(QROWS, QROWS), :] = (score_w - high.astype(F32)).astype(BF16)
    wuv[pl.ds(2 * QROWS, C), :] = vw_v[...].astype(F32).T.astype(BF16)
    stacked = jnp.concatenate(
        [atmos_v[v].astype(F32) for v in range(NATM)] + [jnp.zeros((C - NATM * K, C), F32)], axis=0
    )
    wat[...] = stacked.T.astype(BF16)
    wsurf[...] = jnp.concatenate([surf_v[:, f, :].astype(F32) for f in range(NSURF)], axis=0).astype(BF16)

    for n in range(LEV):
        l = 4 * (n % 3) + n // 3
        biasb[n] = jnp.broadcast_to(bias_v[pl.ds(l, 1), :], (LANES, C)).T
    xs[pl.ds(C - 16, 16), :] = jnp.zeros((16, LEV * LANES), BF16)

    def unpack(s, carry):
        lane = lax.broadcasted_iota(jnp.int32, (16, LANES), 1)
        for t in range(KT):
            g, off = divmod(8 * REST * t, LANES)
            x = recv[rest_raw, s, 16 * g : 16 * g + 16, :]
            if off:
                x = pltpu.roll(x, LANES - off, 1)
            if off + 8 * REST > LANES:
                y = pltpu.roll(recv[rest_raw, s, 16 * g + 16 : 16 * g + 32, :], LANES - off, 1)
                x = jnp.where(lane < LANES - off, x, y)
            recv[rest_done, s, 16 * t : 16 * t + 16, :] = x
        return carry

    def gather(place, j):
        for s in range(1, NDEV):
            v, g = divmod(s - 1, 3)
            xs[pl.ds(K * v, K), pl.ds((3 * j + g) * LANES, LANES)] = recv[place, s, pl.ds(K * j, K), :]

    def embed(first, count):
        cols = pl.ds(first * LANES, count * LANES)
        levels = jnp.dot(wat[...], xs[:, cols], preferred_element_type=F32)
        levels = levels + jnp.concatenate([biasb[first + i] for i in range(count)], axis=1)
        centred = levels - jnp.sum(levels, axis=0, keepdims=True) * (1.0 / C)
        var = jnp.sum(centred * centred, axis=0, keepdims=True) * (1.0 / C)
        xs[:, cols] = (centred * lax.rsqrt(var + 1e-5)).astype(BF16)

    def attend(first, count):
        got = jnp.dot(wuv[...], xs[:, pl.ds(first * LANES, count * LANES)], preferred_element_type=F32)
        for i in range(count):
            part = got[:, i * LANES : (i + 1) * LANES]
            scores[first + i] = part[:QROWS] + part[QROWS : 2 * QROWS]
            vals[first + i] = part[2 * QROWS :].astype(BF16).astype(F32)

    def softmax():
        top = scores[0]
        for l in range(1, LEV):
            top = jnp.maximum(top, scores[l])
        total = jnp.zeros((QROWS, LANES), F32)
        for l in range(LEV):
            e = jnp.exp(scores[l] - top)
            scores[l] = e
            total = total + e
        for l in range(LEV):
            scores[l] = (scores[l] / total).astype(BF16).astype(F32)

    def lay_out(t, turn):
        def move(j, carry):
            start = pl.multiple_of(A * lax.rem(j + turn, BLK), A)
            for a in range(A):
                staged[a, BLK * t + j] = slots[start + a].astype(BF16)
            return carry
        lax.fori_loop(0, BLK, move, 0, unroll=2)

    def arrived(c, start, stop, sem, own_sem):
        whole = recv.at[c, pl.ds(0, NDEV - 1), pl.ds(start, stop - start)]
        pltpu.make_async_copy(whole, whole, sem).wait()
        own(c, start, stop, own_sem).wait()

    def process(t, carry):
        is_rest = t // LAST
        place = t + is_rest * (rest_done - LAST)

        @pl.when(t < LAST)
        def _():
            arrived(t, 0, ROWS, recv_sem.at[t], self_sem.at[t])

        @pl.when(t == LAST)
        def _():
            arrived(FULL, 0, REST_ROWS, recv_sem.at[FULL], self_sem.at[FULL])
            lax.fori_loop(0, NDEV, unpack, 0, unroll=2)

        for j in range(FPD):
            gather(place, j)
        for p in range(LEV // 2):
            embed(2 * p, 2)
        for p in range(LEV // 2):
            attend(2 * p, 2)
        softmax()
        mixture([(l, vals.at[l]) for l in range(LEV)], scores, mix)
        project(recv.at[place, 0], mix, wsurf, ow_v, lat_v, slots)
        lay_out(t, me * (1 - is_rest))
        return carry
    lax.fori_loop(0, FULL, process, 0)

    def piece(i):
        start, stop = PIECES[i]
        arrived(LAST, start, stop, piece_sem.at[i], self_sem.at[FULL + 1 + i])
        rows = pl.ds(start, stop - start)
        last_surf[rows, :] = recv[LAST, 0, rows, :]

    early = LEV - 3
    piece(0)
    for j in range(2):
        gather(LAST, j)
    for p in range(3):
        embed(2 * p, 2)
    for p in range(3):
        attend(2 * p, 2)
    piece(1)
    gather(LAST, 2)
    embed(6, 3)
    attend(6, 3)
    top = scores[0]
    for l in range(1, early):
        top = jnp.maximum(top, scores[l])
    total = jnp.zeros((QROWS, LANES), F32)
    for l in range(early):
        e = jnp.exp(scores[l] - top)
        scores[l] = e
        total = total + e
    mixture([(l, vals.at[l]) for l in range(early)], scores, part)
    scores[0] = top
    scores[1] = total

    piece(2)
    gather(LAST, 3)
    embed(early, 3)
    attend(early, 3)
    last = [scores[l] for l in range(early, LEV)]
    top = jnp.maximum(jnp.maximum(last[0], last[1]), jnp.maximum(last[2], scores[0]))
    last = [jnp.exp(x - top) for x in last]
    scale = jnp.exp(scores[0] - top)
    share = 1.0 / (last[0] + last[1] + last[2] + scale * scores[1])
    scores[0] = scale * share
    for i, e in enumerate(last):
        scores[early + i] = e * share
    mixture([(0, lambda m: part.at[m])] + [(l, vals.at[l]) for l in range(early, LEV)], scores, mix)

    for c in range(FULL + 1):
        whole = send.at[c, pl.ds(0, NDEV - 1), pl.ds(0, ROWS if c < FULL else REST_ROWS)]
        pltpu.make_async_copy(whole, whole, send_sem.at[c]).wait()


def finish(staged, mix, last_surf, wsurf, ow, lat, out_ref, slots, outb, sem):
    ahead = BLK * LAST
    writes = [
        pltpu.make_async_copy(staged.at[:, pl.ds(0, ahead)], out_ref.at[:, pl.ds(0, ahead)], sem.at[0]),
        pltpu.make_async_copy(staged.at[:, pl.ds(ahead, REST)], out_ref.at[:, pl.ds(BLK * FULL, REST)], sem.at[1]),
    ]
    for write in writes:
        write.start()
    project(last_surf, mix, wsurf, ow, lat, slots)

    def move(j, carry):
        start = pl.multiple_of(A * j, A)
        for a in range(A):
            outb[a, j] = slots[start + a].astype(BF16)
        return carry
    half = BLK // 2
    for i in range(2):
        lax.fori_loop(half * i, half * (i + 1), move, 0, unroll=4)
        writes.append(pltpu.make_async_copy(
            outb.at[:, pl.ds(half * i, half)], out_ref.at[:, pl.ds(ahead + half * i, half)], sem.at[2 + i]))
        writes[-1].start()
    for write in writes:
        write.wait()


def shards(fields, surf_weight, atmos_weight, level_bias_table, latents, query_matrix, key_weight, value_weight, out_weight):
    by_token = jnp.transpose(fields, (1, 2, 0))
    surf_cells = jnp.transpose(surf_weight, (1, 0, 2))
    operands = (
        by_token, surf_cells, atmos_weight, level_bias_table, latents,
        query_matrix, key_weight, value_weight, out_weight,
    )
    in_hbm = pl.BlockSpec(memory_space=pl.ANY)
    in_vmem = pl.BlockSpec(memory_space=pltpu.VMEM)
    dma = pltpu.SemaphoreType.DMA
    handed = pl.pallas_call(
        kernel,
        out_shape=[
            pltpu.VMEM((A, EARLY, LATENT + 1, C), BF16),
            pltpu.VMEM((LATENT, C, LANES), BF16),
            pltpu.VMEM((ROWS, LANES), BF16),
            pltpu.VMEM((NSURF * K, C), BF16),
            pltpu.VMEM((C, C), BF16),
            pltpu.VMEM((LATENT, C), BF16),
        ],
        in_specs=[in_hbm] * 9,
        out_specs=[in_vmem] * 6,
        scratch_shapes=[
            pltpu.VMEM((COLS, ROWS, LANES), BF16),
            pltpu.VMEM((FULL + 1, NDEV, ROWS, LANES), BF16),
            pltpu.VMEM((FULL + 2, NDEV, ROWS, LANES), BF16),
            pltpu.VMEM((C, LEV * LANES), BF16),
            pltpu.VMEM((C, C), BF16),
            pltpu.VMEM((C + 2 * QROWS, C), BF16),
            pltpu.VMEM((LEV, C, LANES), F32),
            pltpu.VMEM((LEV, C, LANES), F32),
            pltpu.VMEM((LEV, QROWS, LANES), F32),
            pltpu.VMEM((LATENT, C, LANES), F32),
            pltpu.VMEM((LANES, LATENT + 1, C), F32),
            pltpu.VMEM(surf_cells.shape, BF16),
            pltpu.VMEM(atmos_weight.shape, BF16),
            pltpu.VMEM(level_bias_table.shape, F32),
            pltpu.VMEM(query_matrix.shape, BF16),
            pltpu.VMEM(key_weight.shape, BF16),
            pltpu.VMEM(value_weight.shape, BF16),
            dma((FULL + 2,)),
            dma((8,)),
            dma((FULL + 1,)),
            dma((FULL + 1,)),
            dma((len(PIECES),)),
            dma((FULL + 1 + len(PIECES),)),
        ],
        compiler_params=pltpu.CompilerParams(
            collective_id=0, has_side_effects=True, vmem_limit_bytes=48 * 2**20
        ),
        name="exchange_and_encode",
    )(*[pltpu.with_memory_space_constraint(x, pltpu.HBM) for x in operands])
    return pl.pallas_call(
        finish,
        out_shape=jax.ShapeDtypeStruct((A, COLS, LATENT + 1, C), BF16),
        in_specs=[in_vmem] * 6,
        out_specs=in_hbm,
        scratch_shapes=[
            pltpu.VMEM((LANES, LATENT + 1, C), F32),
            pltpu.VMEM((A, BLK, LATENT + 1, C), BF16),
            dma((4,)),
        ],
        compiler_params=pltpu.CompilerParams(vmem_limit_bytes=8 * 2**20),
        name="finish",
    )(*[pltpu.with_memory_space_constraint(x, pltpu.VMEM) for x in handed])


def solution(mesh):
    in_specs = (P(None, "lon", "lat"), P(), P(), P(), P(), P(), P(), P(), P())
    out_specs = P("lat", "lon", None, None)
    return jax.shard_map(shards, mesh=mesh, in_specs=in_specs, out_specs=out_specs, check_vma=False)
```

```python
import functools
import math

import jax
import jax.numpy as jnp
from jax import lax
from jax.experimental import pallas as pl
from jax.experimental.pallas import tpu as pltpu
from jax.sharding import PartitionSpec as P

C = 512
HEADS = 16
HEAD_CHANNELS = 32
K = 100
NSURF = 4
NATM = 5
LATENT = 3
LEV = 12
NDEV = 16
FPD = 4
ROWS = 400
A = 8
COLS = 90
LANES = 128
BLK = 16
FULL = 5
REST = 10
REST_ROWS = 256
KT = 25
QROWS = LATENT * HEADS
LAST = FULL - 1
OPENING = 80
PIECES = ((0, 208), (208, 400))
EARLY_LEVELS = 6
EARLY = 5 * BLK

MESH = pl.DeviceIdType.MESH
BF16 = jnp.bfloat16
F32 = jnp.float32


def far_first():
    offsets = [(dy, dz, dc) for dy in range(4) for dz in range(2) for dc in range(2)][1:]
    return sorted(offsets, key=lambda o: -(min(o[0], 4 - o[0]) + o[1]))


OFFSETS = far_first()
FAR = [o for o in OFFSETS if min(o[0], 4 - o[0]) + o[1] >= 2]
NEAR = [o for o in OFFSETS if o not in FAR]


def peer_of(me, offset):
    dy, dz, dc = offset
    y, z, c = me // 4, (me // 2) % 2, me % 2
    return ((y + dy) % 4) * 4 + ((z + dz) % 2) * 2 + (c + dc) % 2


def block_transpose(parts):
    lane = lax.broadcasted_iota(jnp.int32, parts[0].shape, 1)
    turned = [x if j == 0 else pltpu.roll(x, 8 * j, 1) for j, x in enumerate(parts)]
    held = [turned[-e % BLK] for e in range(BLK)]
    for s in (1, 2, 4, 8):
        mask = (lane & (8 * s)) != 0
        held = [jnp.where(mask, held[(e - s) % BLK], held[e]) for e in range(BLK)]
    return held


def mixture(terms, shares, out):
    for h in range(HEADS):
        rows = pl.ds(HEAD_CHANNELS * h, HEAD_CHANNELS)
        sums = [None] * LATENT
        for i, values in terms:
            held = [values(m)[rows, :] for m in range(LATENT)] if callable(values) else [values[rows, :]] * LATENT
            for m in range(LATENT):
                term = shares[i, pl.ds(m * HEADS + h, 1), :] * held[m]
                sums[m] = term if sums[m] is None else sums[m] + term
        for m in range(LATENT):
            out[m, rows, :] = sums[m].astype(out.dtype)


def project(block, mix, wsurf, ow, lat, slots):
    contract = (((0,), (0,)), ((), ()))
    slots[:, 0, :] = lax.dot_general(block[...], wsurf[...], contract, preferred_element_type=F32)
    for m in range(LATENT):
        agg = lax.dot_general(mix[m], ow[...], contract, preferred_element_type=F32)
        slots[:, m + 1, :] = agg + lat[pl.ds(m, 1), :].astype(F32)


def kernel(
    fields_ref, surf_ref, atmos_ref, bias_ref, lat_ref, qm_ref, kw_ref, vw_ref, ow_ref,
    staged, mix, last_surf, wsurf, ow_v, lat_v,
    inb, send, recv, xs, wat, wuv, biasb, vals, scores, part, slots,
    surf_v, atmos_v, bias_v, qm_v, kw_v, vw_v,
    in_sem, w_sem, send_sem, recv_sem, piece_sem, self_sem,
):
    me = lax.axis_index("lat")
    rest_raw, rest_done = FULL, FULL + 1

    def load(c, n=BLK, start=0, stop=ROWS, sem=None):
        here, rows = pl.ds(BLK * c, n), pl.ds(start, stop - start)
        return pltpu.make_async_copy(
            fields_ref.at[here, rows], inb.at[here, rows], in_sem.at[c if sem is None else sem])

    load(0, stop=OPENING).start()
    barrier = pltpu.get_barrier_semaphore()
    for o in OFFSETS:
        pl.semaphore_signal(barrier, inc=1, device_id={"lat": peer_of(me, o)}, device_id_type=MESH)
    load(0, start=OPENING, sem=FULL + 1).start()
    for c in range(1, FULL):
        load(c).start()
    load(FULL, REST).start()
    weight_loads = []
    for i, (src, dst) in enumerate((
        (qm_ref, qm_v), (lat_ref, lat_v), (kw_ref, kw_v), (vw_ref, vw_v), (atmos_ref, atmos_v),
        (surf_ref, surf_v), (bias_ref, bias_v), (ow_ref, ow_v),
    )):
        weight_loads.append(pltpu.make_async_copy(src, dst, w_sem.at[i]))
        weight_loads[-1].start()

    def unturn(e, y):
        return y if e == 0 else pltpu.roll(y, LANES - 8 * e, 1)

    def shuffle_full(c, straight=False, start=0, stop=ROWS):
        def tile(t, carry):
            rows = pl.ds(pl.multiple_of(16 * t, 16), 16)
            parts = [inb[BLK * c + j, rows, :] for j in range(BLK)]
            for e, y in enumerate(block_transpose(parts)):
                send[c, e, rows, :] = unturn(e, y) if straight else y
            return carry
        lax.fori_loop(start // 16, stop // 16, tile, 0, unroll=5)

    def rest_group(q, g, count):
        parts = []
        for j in range(BLK):
            t, b = divmod(BLK * g + j, REST) if j < count else (0, j - count)
            rows = pl.ds(pl.multiple_of(128 * q + 16 * t, 16), 16)
            parts.append(inb[BLK * FULL + b, rows, :])
        rows = pl.ds(pl.multiple_of(80 * q + 16 * g, 16), 16)
        for e, y in enumerate(block_transpose(parts)):
            send[FULL, e, rows, :] = unturn(e, y)

    def shuffle_rest():
        def five(q, carry):
            for g in range(5):
                rest_group(q, g, BLK)
            return carry
        lax.fori_loop(0, 3, five, 0)
        rest_group(3, 0, REST)

    def own(c, start, stop, sem):
        rows = pl.ds(start, stop - start)
        return pltpu.make_async_copy(send.at[c, me, rows], recv.at[c, me, rows], sem)

    def ship(c, start, stop, sem, own_sem, offsets=OFFSETS):
        rows = pl.ds(start, stop - start)
        for o in offsets:
            d = peer_of(me, o)
            pltpu.make_async_remote_copy(
                src_ref=send.at[c, d, rows], dst_ref=recv.at[c, me, rows],
                send_sem=send_sem.at[c], recv_sem=sem,
                device_id={"lat": d}, device_id_type=MESH,
            ).start()
        if own_sem is not None:
            own(c, start, stop, own_sem).start()

    def ship_whole(c, rows):
        ship(c, 0, rows, recv_sem.at[c], self_sem.at[c])

    load(0, stop=OPENING).wait()
    shuffle_full(0, stop=OPENING)
    pl.semaphore_wait(barrier, NDEV - 1)
    ship(0, 0, OPENING, recv_sem.at[0], self_sem.at[0])
    load(0, start=OPENING, sem=FULL + 1).wait()
    shuffle_full(0, start=OPENING)
    ship(0, OPENING, ROWS, recv_sem.at[0], self_sem.at[0])

    def send_next(c, carry):
        load(c).wait()
        shuffle_full(c)
        ship_whole(c, ROWS)
        return carry
    lax.fori_loop(1, LAST, send_next, 0)
    load(FULL, REST).wait()
    shuffle_rest()
    ship_whole(FULL, REST_ROWS)
    load(LAST).wait()
    shuffle_full(LAST, straight=True)
    for o in FAR:
        for i, (start, stop) in enumerate(PIECES):
            ship(LAST, start, stop, piece_sem.at[i], None, [o])
    for i, (start, stop) in enumerate(PIECES):
        ship(LAST, start, stop, piece_sem.at[i], self_sem.at[FULL + 1 + i], NEAR)

    for w in weight_loads:
        w.wait()
    queries = jnp.dot(lat_v[...], qm_v[...], preferred_element_type=F32).astype(BF16).astype(F32)
    channel_head = lax.broadcasted_iota(jnp.int32, (HEADS, C), 1) // HEAD_CHANNELS
    own_head = channel_head == lax.broadcasted_iota(jnp.int32, (HEADS, C), 0)
    spread = jnp.concatenate(
        [jnp.where(own_head, jnp.broadcast_to(queries[m : m + 1], (HEADS, C)), 0.0) for m in range(LATENT)],
        axis=0,
    ).astype(BF16)
    score_w = lax.dot_general(
        spread, kw_v[...], (((1,), (1,)), ((), ())), preferred_element_type=F32
    ) * (1.0 / math.sqrt(HEAD_CHANNELS))
    high = score_w.astype(BF16)
    wuv[pl.ds(0, QROWS), :] = high
    wuv[pl.ds(QROWS, QROWS), :] = (score_w - high.astype(F32)).astype(BF16)
    wuv[pl.ds(2 * QROWS, C), :] = vw_v[...].astype(F32).T.astype(BF16)
    stacked = jnp.concatenate(
        [atmos_v[v].astype(F32) for v in range(NATM)] + [jnp.zeros((C - NATM * K, C), F32)], axis=0
    )
    wat[...] = stacked.T.astype(BF16)
    wsurf[...] = jnp.concatenate([surf_v[:, f, :].astype(F32) for f in range(NSURF)], axis=0).astype(BF16)

    for n in range(LEV):
        l = 4 * (n % 3) + n // 3
        biasb[n] = jnp.broadcast_to(bias_v[pl.ds(l, 1), :], (LANES, C)).T
    xs[pl.ds(C - 16, 16), :] = jnp.zeros((16, LEV * LANES), BF16)

    def unpack(s, carry):
        lane = lax.broadcasted_iota(jnp.int32, (16, LANES), 1)
        for t in range(KT):
            g, off = divmod(8 * REST * t, LANES)
            x = recv[rest_raw, s, 16 * g : 16 * g + 16, :]
            if off:
                x = pltpu.roll(x, LANES - off, 1)
            if off + 8 * REST > LANES:
                y = pltpu.roll(recv[rest_raw, s, 16 * g + 16 : 16 * g + 32, :], LANES - off, 1)
                x = jnp.where(lane < LANES - off, x, y)
            recv[rest_done, s, 16 * t : 16 * t + 16, :] = x
        return carry

    def gather(place, j):
        for s in range(1, NDEV):
            v, g = divmod(s - 1, 3)
            xs[pl.ds(K * v, K), pl.ds((3 * j + g) * LANES, LANES)] = recv[place, s, pl.ds(K * j, K), :]

    def embed(first, count):
        cols = pl.ds(first * LANES, count * LANES)
        levels = jnp.dot(wat[...], xs[:, cols], preferred_element_type=F32)
        levels = levels + jnp.concatenate([biasb[first + i] for i in range(count)], axis=1)
        centred = levels - jnp.sum(levels, axis=0, keepdims=True) * (1.0 / C)
        var = jnp.sum(centred * centred, axis=0, keepdims=True) * (1.0 / C)
        xs[:, cols] = (centred * lax.rsqrt(var + 1e-5)).astype(BF16)

    def attend(first, count):
        got = jnp.dot(wuv[...], xs[:, pl.ds(first * LANES, count * LANES)], preferred_element_type=F32)
        for i in range(count):
            part = got[:, i * LANES : (i + 1) * LANES]
            scores[first + i] = part[:QROWS] + part[QROWS : 2 * QROWS]
            vals[first + i] = part[2 * QROWS :].astype(BF16).astype(F32)

    def softmax():
        top = scores[0]
        for l in range(1, LEV):
            top = jnp.maximum(top, scores[l])
        total = jnp.zeros((QROWS, LANES), F32)
        for l in range(LEV):
            e = jnp.exp(scores[l] - top)
            scores[l] = e
            total = total + e
        for l in range(LEV):
            scores[l] = (scores[l] / total).astype(BF16).astype(F32)

    def lay_out(t, turn):
        def move(j, carry):
            start = pl.multiple_of(A * lax.rem(j + turn, BLK), A)
            for a in range(A):
                staged[a, BLK * t + j] = slots[start + a].astype(BF16)
            return carry
        lax.fori_loop(0, BLK, move, 0, unroll=2)

    def arrived(c, start, stop, sem, own_sem):
        whole = recv.at[c, pl.ds(0, NDEV - 1), pl.ds(start, stop - start)]
        pltpu.make_async_copy(whole, whole, sem).wait()
        own(c, start, stop, own_sem).wait()

    def process(t, carry):
        is_rest = t // LAST
        place = t + is_rest * (rest_done - LAST)

        @pl.when(t < LAST)
        def _():
            arrived(t, 0, ROWS, recv_sem.at[t], self_sem.at[t])

        @pl.when(t == LAST)
        def _():
            arrived(FULL, 0, REST_ROWS, recv_sem.at[FULL], self_sem.at[FULL])
            lax.fori_loop(0, NDEV, unpack, 0, unroll=2)

        for j in range(FPD):
            gather(place, j)
        for p in range(LEV // 2):
            embed(2 * p, 2)
        for p in range(LEV // 2):
            attend(2 * p, 2)
        softmax()
        mixture([(l, vals.at[l]) for l in range(LEV)], scores, mix)
        project(recv.at[place, 0], mix, wsurf, ow_v, lat_v, slots)
        lay_out(t, me * (1 - is_rest))
        return carry
    lax.fori_loop(0, FULL, process, 0)

    def piece(i):
        start, stop = PIECES[i]
        arrived(LAST, start, stop, piece_sem.at[i], self_sem.at[FULL + 1 + i])
        rows = pl.ds(start, stop - start)
        last_surf[rows, :] = recv[LAST, 0, rows, :]

    early = EARLY_LEVELS
    piece(0)
    for j in range(2):
        gather(LAST, j)
    for p in range(0, early, 2):
        embed(p, 2)
    for p in range(0, early, 2):
        attend(p, 2)
    top = scores[0]
    for l in range(1, early):
        top = jnp.maximum(top, scores[l])
    total = jnp.zeros((QROWS, LANES), F32)
    for l in range(early):
        e = jnp.exp(scores[l] - top)
        scores[l] = e
        total = total + e
    mixture([(l, vals.at[l]) for l in range(early)], scores, part)
    scores[0] = top
    scores[1] = total

    piece(1)
    for j in range(2, FPD):
        gather(LAST, j)
    for p in range(early, LEV, 2):
        embed(p, 2)
    for p in range(early, LEV, 2):
        attend(p, 2)
    last = [scores[l] for l in range(early, LEV)]
    top = scores[0]
    for x in last:
        top = jnp.maximum(top, x)
    last = [jnp.exp(x - top) for x in last]
    scale = jnp.exp(scores[0] - top)
    share = 1.0 / (sum(last) + scale * scores[1])
    scores[0] = scale * share
    for i, e in enumerate(last):
        scores[early + i] = e * share
    mixture([(0, lambda m: part.at[m])] + [(l, vals.at[l]) for l in range(early, LEV)], scores, mix)

    for c in range(FULL + 1):
        whole = send.at[c, pl.ds(0, NDEV - 1), pl.ds(0, ROWS if c < FULL else REST_ROWS)]
        pltpu.make_async_copy(whole, whole, send_sem.at[c]).wait()


def finish(staged, mix, last_surf, wsurf, ow, lat, out_ref, slots, outb, sem):
    ahead = BLK * LAST
    writes = [
        pltpu.make_async_copy(staged.at[:, pl.ds(0, ahead)], out_ref.at[:, pl.ds(0, ahead)], sem.at[0]),
        pltpu.make_async_copy(staged.at[:, pl.ds(ahead, REST)], out_ref.at[:, pl.ds(BLK * FULL, REST)], sem.at[1]),
    ]
    for write in writes:
        write.start()
    project(last_surf, mix, wsurf, ow, lat, slots)

    def move(j, carry):
        start = pl.multiple_of(A * j, A)
        for a in range(A):
            outb[a, j] = slots[start + a].astype(BF16)
        return carry
    half = BLK // 2
    for i in range(2):
        lax.fori_loop(half * i, half * (i + 1), move, 0, unroll=4)
        writes.append(pltpu.make_async_copy(
            outb.at[:, pl.ds(half * i, half)], out_ref.at[:, pl.ds(ahead + half * i, half)], sem.at[2 + i]))
        writes[-1].start()
    for write in writes:
        write.wait()


def shards(fields, surf_weight, atmos_weight, level_bias_table, latents, query_matrix, key_weight, value_weight, out_weight):
    by_token = jnp.transpose(fields, (1, 2, 0))
    surf_cells = jnp.transpose(surf_weight, (1, 0, 2))
    operands = (
        by_token, surf_cells, atmos_weight, level_bias_table, latents,
        query_matrix, key_weight, value_weight, out_weight,
    )
    in_hbm = pl.BlockSpec(memory_space=pl.ANY)
    in_vmem = pl.BlockSpec(memory_space=pltpu.VMEM)
    dma = pltpu.SemaphoreType.DMA
    handed = pl.pallas_call(
        kernel,
        out_shape=[
            pltpu.VMEM((A, EARLY, LATENT + 1, C), BF16),
            pltpu.VMEM((LATENT, C, LANES), BF16),
            pltpu.VMEM((ROWS, LANES), BF16),
            pltpu.VMEM((NSURF * K, C), BF16),
            pltpu.VMEM((C, C), BF16),
            pltpu.VMEM((LATENT, C), BF16),
        ],
        in_specs=[in_hbm] * 9,
        out_specs=[in_vmem] * 6,
        scratch_shapes=[
            pltpu.VMEM((COLS, ROWS, LANES), BF16),
            pltpu.VMEM((FULL + 1, NDEV, ROWS, LANES), BF16),
            pltpu.VMEM((FULL + 2, NDEV, ROWS, LANES), BF16),
            pltpu.VMEM((C, LEV * LANES), BF16),
            pltpu.VMEM((C, C), BF16),
            pltpu.VMEM((C + 2 * QROWS, C), BF16),
            pltpu.VMEM((LEV, C, LANES), F32),
            pltpu.VMEM((LEV, C, LANES), F32),
            pltpu.VMEM((LEV, QROWS, LANES), F32),
            pltpu.VMEM((LATENT, C, LANES), F32),
            pltpu.VMEM((LANES, LATENT + 1, C), F32),
            pltpu.VMEM(surf_cells.shape, BF16),
            pltpu.VMEM(atmos_weight.shape, BF16),
            pltpu.VMEM(level_bias_table.shape, F32),
            pltpu.VMEM(query_matrix.shape, BF16),
            pltpu.VMEM(key_weight.shape, BF16),
            pltpu.VMEM(value_weight.shape, BF16),
            dma((FULL + 2,)),
            dma((8,)),
            dma((FULL + 1,)),
            dma((FULL + 1,)),
            dma((len(PIECES),)),
            dma((FULL + 1 + len(PIECES),)),
        ],
        compiler_params=pltpu.CompilerParams(
            collective_id=0, has_side_effects=True, vmem_limit_bytes=48 * 2**20
        ),
        name="exchange_and_encode",
    )(*[pltpu.with_memory_space_constraint(x, pltpu.HBM) for x in operands])
    return pl.pallas_call(
        finish,
        out_shape=jax.ShapeDtypeStruct((A, COLS, LATENT + 1, C), BF16),
        in_specs=[in_vmem] * 6,
        out_specs=in_hbm,
        scratch_shapes=[
            pltpu.VMEM((LANES, LATENT + 1, C), F32),
            pltpu.VMEM((A, BLK, LATENT + 1, C), BF16),
            dma((4,)),
        ],
        compiler_params=pltpu.CompilerParams(vmem_limit_bytes=8 * 2**20),
        name="finish",
    )(*[pltpu.with_memory_space_constraint(x, pltpu.VMEM) for x in handed])


def solution(mesh):
    in_specs = (P(None, "lon", "lat"), P(), P(), P(), P(), P(), P(), P(), P())
    out_specs = P("lat", "lon", None, None)
    return jax.shard_map(shards, mesh=mesh, in_specs=in_specs, out_specs=out_specs, check_vma=False)
```

```python
import functools
import math

import jax
import jax.numpy as jnp
from jax import lax
from jax.experimental import pallas as pl
from jax.experimental.pallas import tpu as pltpu
from jax.sharding import PartitionSpec as P

C = 512
HEADS = 16
HEAD_CHANNELS = 32
K = 100
NSURF = 4
NATM = 5
LATENT = 3
LEV = 12
NDEV = 16
FPD = 4
ROWS = 400
A = 8
COLS = 90
LANES = 128
BLK = 16
FULL = 5
REST = 10
REST_ROWS = 256
KT = 25
QROWS = LATENT * HEADS
LAST = FULL - 1
OPENING = 80
PIECES = ((0, 208), (208, 400))
EARLY_LEVELS = 6
EARLY = 5 * BLK

MESH = pl.DeviceIdType.MESH
BF16 = jnp.bfloat16
F32 = jnp.float32


def far_first():
    offsets = [(dy, dz, dc) for dy in range(4) for dz in range(2) for dc in range(2)][1:]
    return sorted(offsets, key=lambda o: -(min(o[0], 4 - o[0]) + o[1]))


OFFSETS = far_first()
FAR = [o for o in OFFSETS if min(o[0], 4 - o[0]) + o[1] >= 2]
NEAR = [o for o in OFFSETS if o not in FAR]


def peer_of(me, offset):
    dy, dz, dc = offset
    y, z, c = me // 4, (me // 2) % 2, me % 2
    return ((y + dy) % 4) * 4 + ((z + dz) % 2) * 2 + (c + dc) % 2


def block_transpose(parts):
    lane = lax.broadcasted_iota(jnp.int32, parts[0].shape, 1)
    turned = [x if j == 0 else pltpu.roll(x, 8 * j, 1) for j, x in enumerate(parts)]
    held = [turned[-e % BLK] for e in range(BLK)]
    for s in (1, 2, 4, 8):
        mask = (lane & (8 * s)) != 0
        held = [jnp.where(mask, held[(e - s) % BLK], held[e]) for e in range(BLK)]
    return held


def mixture(terms, shares, out):
    for h in range(HEADS):
        rows = pl.ds(HEAD_CHANNELS * h, HEAD_CHANNELS)
        sums = [None] * LATENT
        for i, values in terms:
            held = [values(m)[rows, :] for m in range(LATENT)] if callable(values) else [values[rows, :]] * LATENT
            for m in range(LATENT):
                term = shares[i, pl.ds(m * HEADS + h, 1), :] * held[m]
                sums[m] = term if sums[m] is None else sums[m] + term
        for m in range(LATENT):
            out[rows, pl.ds(m * LANES, LANES)] = sums[m].astype(out.dtype)


def project(block, mix, wsurf, ow, lat, slots):
    contract = (((0,), (0,)), ((), ()))
    slots[:, 0, :] = lax.dot_general(block[...], wsurf[...], contract, preferred_element_type=F32)
    agg = lax.dot_general(mix[...], ow[...], contract, preferred_element_type=F32)
    for m in range(LATENT):
        slots[:, m + 1, :] = agg[m * LANES : (m + 1) * LANES] + lat[pl.ds(m, 1), :].astype(F32)


def kernel(
    fields_ref, surf_ref, atmos_ref, bias_ref, lat_ref, qm_ref, kw_ref, vw_ref, ow_ref,
    staged, vals, scores, part, last_surf, wsurf, ow_v, lat_v,
    inb, send, recv, xs, wat, wuv, biasb, mix, slots,
    surf_v, atmos_v, bias_v, qm_v, kw_v, vw_v,
    in_sem, w_sem, send_sem, recv_sem, piece_sem, self_sem,
):
    me = lax.axis_index("lat")
    rest_raw, rest_done = FULL, FULL + 1

    def load(c, n=BLK, start=0, stop=ROWS, sem=None):
        here, rows = pl.ds(BLK * c, n), pl.ds(start, stop - start)
        return pltpu.make_async_copy(
            fields_ref.at[here, rows], inb.at[here, rows], in_sem.at[c if sem is None else sem])

    load(0, stop=OPENING).start()
    barrier = pltpu.get_barrier_semaphore()
    for o in OFFSETS:
        pl.semaphore_signal(barrier, inc=1, device_id={"lat": peer_of(me, o)}, device_id_type=MESH)
    load(0, start=OPENING, sem=FULL + 1).start()
    def unturn(e, y):
        return y if e == 0 else pltpu.roll(y, LANES - 8 * e, 1)

    def shuffle_full(c, straight=False, start=0, stop=ROWS):
        def tile(t, carry):
            rows = pl.ds(pl.multiple_of(16 * t, 16), 16)
            parts = [inb[BLK * c + j, rows, :] for j in range(BLK)]
            for e, y in enumerate(block_transpose(parts)):
                send[c, e, rows, :] = unturn(e, y) if straight else y
            return carry
        lax.fori_loop(start // 16, stop // 16, tile, 0, unroll=5)

    def rest_group(q, g, count):
        parts = []
        for j in range(BLK):
            t, b = divmod(BLK * g + j, REST) if j < count else (0, j - count)
            rows = pl.ds(pl.multiple_of(128 * q + 16 * t, 16), 16)
            parts.append(inb[BLK * FULL + b, rows, :])
        rows = pl.ds(pl.multiple_of(80 * q + 16 * g, 16), 16)
        for e, y in enumerate(block_transpose(parts)):
            send[FULL, e, rows, :] = unturn(e, y)

    def shuffle_rest():
        def five(q, carry):
            for g in range(5):
                rest_group(q, g, BLK)
            return carry
        lax.fori_loop(0, 3, five, 0)
        rest_group(3, 0, REST)

    def own(c, start, stop, sem):
        rows = pl.ds(start, stop - start)
        return pltpu.make_async_copy(send.at[c, me, rows], recv.at[c, me, rows], sem)

    def ship(c, start, stop, sem, own_sem, offsets=OFFSETS):
        rows = pl.ds(start, stop - start)
        for o in offsets:
            d = peer_of(me, o)
            pltpu.make_async_remote_copy(
                src_ref=send.at[c, d, rows], dst_ref=recv.at[c, me, rows],
                send_sem=send_sem.at[c], recv_sem=sem,
                device_id={"lat": d}, device_id_type=MESH,
            ).start()
        if own_sem is not None:
            own(c, start, stop, own_sem).start()

    def ship_whole(c, rows):
        ship(c, 0, rows, recv_sem.at[c], self_sem.at[c])

    load(0, stop=OPENING).wait()
    shuffle_full(0, stop=OPENING)
    pl.semaphore_wait(barrier, NDEV - 1)
    ship(0, 0, OPENING, recv_sem.at[0], self_sem.at[0])
    for c in range(1, FULL):
        load(c).start()
    load(FULL, REST).start()
    load(0, start=OPENING, sem=FULL + 1).wait()
    shuffle_full(0, start=OPENING)
    ship(0, OPENING, ROWS, recv_sem.at[0], self_sem.at[0])
    weight_loads = []
    for i, (src, dst) in enumerate((
        (qm_ref, qm_v), (lat_ref, lat_v), (kw_ref, kw_v), (vw_ref, vw_v), (atmos_ref, atmos_v),
        (surf_ref, surf_v), (bias_ref, bias_v), (ow_ref, ow_v),
    )):
        weight_loads.append(pltpu.make_async_copy(src, dst, w_sem.at[i]))
        weight_loads[-1].start()

    def send_next(c, carry):
        load(c).wait()
        shuffle_full(c)
        ship_whole(c, ROWS)
        return carry
    lax.fori_loop(1, LAST, send_next, 0)
    load(FULL, REST).wait()
    shuffle_rest()
    ship_whole(FULL, REST_ROWS)
    load(LAST).wait()
    shuffle_full(LAST, straight=True)
    for o in FAR:
        for i, (start, stop) in enumerate(PIECES):
            ship(LAST, start, stop, piece_sem.at[i], None, [o])
    for i, (start, stop) in enumerate(PIECES):
        ship(LAST, start, stop, piece_sem.at[i], self_sem.at[FULL + 1 + i], NEAR)

    for w in weight_loads:
        w.wait()
    queries = jnp.dot(lat_v[...], qm_v[...], preferred_element_type=F32).astype(BF16).astype(F32)
    channel_head = lax.broadcasted_iota(jnp.int32, (HEADS, C), 1) // HEAD_CHANNELS
    own_head = channel_head == lax.broadcasted_iota(jnp.int32, (HEADS, C), 0)
    spread = jnp.concatenate(
        [jnp.where(own_head, jnp.broadcast_to(queries[m : m + 1], (HEADS, C)), 0.0) for m in range(LATENT)],
        axis=0,
    ).astype(BF16)
    score_w = lax.dot_general(
        spread, kw_v[...], (((1,), (1,)), ((), ())), preferred_element_type=F32
    ) * (1.0 / math.sqrt(HEAD_CHANNELS))
    high = score_w.astype(BF16)
    wuv[pl.ds(0, QROWS), :] = high
    wuv[pl.ds(QROWS, QROWS), :] = (score_w - high.astype(F32)).astype(BF16)
    wuv[pl.ds(2 * QROWS, C), :] = vw_v[...].astype(F32).T.astype(BF16)
    stacked = jnp.concatenate(
        [atmos_v[v].astype(F32) for v in range(NATM)] + [jnp.zeros((C - NATM * K, C), F32)], axis=0
    )
    wat[...] = stacked.T.astype(BF16)
    wsurf[...] = jnp.concatenate([surf_v[:, f, :].astype(F32) for f in range(NSURF)], axis=0).astype(BF16)

    for n in range(LEV):
        l = 4 * (n % 3) + n // 3
        biasb[n] = jnp.broadcast_to(bias_v[pl.ds(l, 1), :], (LANES, C)).T
    xs[pl.ds(C - 16, 16), :] = jnp.zeros((16, LEV * LANES), BF16)

    def unpack(s, carry):
        lane = lax.broadcasted_iota(jnp.int32, (16, LANES), 1)
        for t in range(KT):
            g, off = divmod(8 * REST * t, LANES)
            x = recv[rest_raw, s, 16 * g : 16 * g + 16, :]
            if off:
                x = pltpu.roll(x, LANES - off, 1)
            if off + 8 * REST > LANES:
                y = pltpu.roll(recv[rest_raw, s, 16 * g + 16 : 16 * g + 32, :], LANES - off, 1)
                x = jnp.where(lane < LANES - off, x, y)
            recv[rest_done, s, 16 * t : 16 * t + 16, :] = x
        return carry

    def gather(place, j):
        for s in range(1, NDEV):
            v, g = divmod(s - 1, 3)
            xs[pl.ds(K * v, K), pl.ds((3 * j + g) * LANES, LANES)] = recv[place, s, pl.ds(K * j, K), :]

    def embed(first, count):
        cols = pl.ds(first * LANES, count * LANES)
        levels = jnp.dot(wat[...], xs[:, cols], preferred_element_type=F32)
        levels = levels + jnp.concatenate([biasb[first + i] for i in range(count)], axis=1)
        centred = levels - jnp.sum(levels, axis=0, keepdims=True) * (1.0 / C)
        var = jnp.sum(centred * centred, axis=0, keepdims=True) * (1.0 / C)
        xs[:, cols] = (centred * lax.rsqrt(var + 1e-5)).astype(BF16)

    def attend(first, count):
        got = jnp.dot(wuv[...], xs[:, pl.ds(first * LANES, count * LANES)], preferred_element_type=F32)
        for i in range(count):
            part = got[:, i * LANES : (i + 1) * LANES]
            scores[first + i] = part[:QROWS] + part[QROWS : 2 * QROWS]
            vals[first + i] = part[2 * QROWS :].astype(BF16).astype(F32)

    def softmax():
        top = scores[0]
        for l in range(1, LEV):
            top = jnp.maximum(top, scores[l])
        total = jnp.zeros((QROWS, LANES), F32)
        for l in range(LEV):
            e = jnp.exp(scores[l] - top)
            scores[l] = e
            total = total + e
        for l in range(LEV):
            scores[l] = (scores[l] / total).astype(BF16).astype(F32)

    def lay_out(t, turn):
        def move(j, carry):
            start = pl.multiple_of(A * lax.rem(j + turn, BLK), A)
            for a in range(A):
                staged[a, BLK * t + j] = slots[start + a].astype(BF16)
            return carry
        lax.fori_loop(0, BLK, move, 0, unroll=2)

    def arrived(c, start, stop, sem, own_sem):
        whole = recv.at[c, pl.ds(0, NDEV - 1), pl.ds(start, stop - start)]
        pltpu.make_async_copy(whole, whole, sem).wait()
        own(c, start, stop, own_sem).wait()

    def process(t, carry):
        is_rest = t // LAST
        place = t + is_rest * (rest_done - LAST)

        @pl.when(t < LAST)
        def _():
            arrived(t, 0, ROWS, recv_sem.at[t], self_sem.at[t])

        @pl.when(t == LAST)
        def _():
            arrived(FULL, 0, REST_ROWS, recv_sem.at[FULL], self_sem.at[FULL])
            lax.fori_loop(0, NDEV, unpack, 0, unroll=2)

        for j in range(FPD):
            gather(place, j)
        for p in range(LEV // 2):
            embed(2 * p, 2)
        for p in range(LEV // 2):
            attend(2 * p, 2)
        softmax()
        mixture([(l, vals.at[l]) for l in range(LEV)], scores, mix)
        project(recv.at[place, 0], mix, wsurf, ow_v, lat_v, slots)
        lay_out(t, me * (1 - is_rest))
        return carry
    lax.fori_loop(0, FULL, process, 0)

    def piece(i):
        start, stop = PIECES[i]
        arrived(LAST, start, stop, piece_sem.at[i], self_sem.at[FULL + 1 + i])
        rows = pl.ds(start, stop - start)
        last_surf[rows, :] = recv[LAST, 0, rows, :]

    early = EARLY_LEVELS
    piece(0)
    for j in range(2):
        gather(LAST, j)
    for p in range(0, early, 2):
        embed(p, 2)
    for p in range(0, early, 2):
        attend(p, 2)
    top = scores[0]
    for l in range(1, early):
        top = jnp.maximum(top, scores[l])
    total = jnp.zeros((QROWS, LANES), F32)
    for l in range(early):
        e = jnp.exp(scores[l] - top)
        scores[l] = e
        total = total + e
    mixture([(l, vals.at[l]) for l in range(early)], scores, part)
    scores[0] = top
    scores[1] = total

    piece(1)
    for j in range(2, FPD):
        gather(LAST, j)
    for p in range(early, LEV, 2):
        embed(p, 2)
    for p in range(early, LEV, 2):
        attend(p, 2)
    last = [scores[l] for l in range(early, LEV)]
    top = scores[0]
    for x in last:
        top = jnp.maximum(top, x)
    last = [jnp.exp(x - top) for x in last]
    scale = jnp.exp(scores[0] - top)
    share = 1.0 / (sum(last) + scale * scores[1])
    scores[0] = scale * share
    for i, e in enumerate(last):
        scores[early + i] = e * share

    for c in range(FULL + 1):
        whole = send.at[c, pl.ds(0, NDEV - 1), pl.ds(0, ROWS if c < FULL else REST_ROWS)]
        pltpu.make_async_copy(whole, whole, send_sem.at[c]).wait()


def finish(staged, vals, scores, part, last_surf, wsurf, ow, lat, out_ref, mix, slots, outb, sem):
    ahead = BLK * LAST
    writes = [
        pltpu.make_async_copy(staged.at[:, pl.ds(0, ahead)], out_ref.at[:, pl.ds(0, ahead)], sem.at[0]),
        pltpu.make_async_copy(staged.at[:, pl.ds(ahead, REST)], out_ref.at[:, pl.ds(BLK * FULL, REST)], sem.at[1]),
    ]
    for write in writes:
        write.start()
    mixture([(0, lambda m: part.at[:, pl.ds(m * LANES, LANES)])] + [(l, vals.at[l]) for l in range(EARLY_LEVELS, LEV)], scores, mix)
    project(last_surf, mix, wsurf, ow, lat, slots)

    def move(j, carry):
        start = pl.multiple_of(A * j, A)
        for a in range(A):
            outb[a, j] = slots[start + a].astype(BF16)
        return carry
    half = BLK // 2
    for i in range(2):
        lax.fori_loop(half * i, half * (i + 1), move, 0, unroll=4)
        writes.append(pltpu.make_async_copy(
            outb.at[:, pl.ds(half * i, half)], out_ref.at[:, pl.ds(ahead + half * i, half)], sem.at[2 + i]))
        writes[-1].start()
    for write in writes:
        write.wait()


def shards(fields, surf_weight, atmos_weight, level_bias_table, latents, query_matrix, key_weight, value_weight, out_weight):
    by_token = jnp.transpose(fields, (1, 2, 0))
    surf_cells = jnp.transpose(surf_weight, (1, 0, 2))
    operands = (
        by_token, surf_cells, atmos_weight, level_bias_table, latents,
        query_matrix, key_weight, value_weight, out_weight,
    )
    in_hbm = pl.BlockSpec(memory_space=pl.ANY)
    in_vmem = pl.BlockSpec(memory_space=pltpu.VMEM)
    dma = pltpu.SemaphoreType.DMA
    handed = pl.pallas_call(
        kernel,
        out_shape=[
            pltpu.VMEM((A, EARLY, LATENT + 1, C), BF16),
            pltpu.VMEM((LEV, C, LANES), F32),
            pltpu.VMEM((LEV, QROWS, LANES), F32),
            pltpu.VMEM((C, LATENT * LANES), F32),
            pltpu.VMEM((ROWS, LANES), BF16),
            pltpu.VMEM((NSURF * K, C), BF16),
            pltpu.VMEM((C, C), BF16),
            pltpu.VMEM((LATENT, C), BF16),
        ],
        in_specs=[in_hbm] * 9,
        out_specs=[in_vmem] * 8,
        scratch_shapes=[
            pltpu.VMEM((COLS, ROWS, LANES), BF16),
            pltpu.VMEM((FULL + 1, NDEV, ROWS, LANES), BF16),
            pltpu.VMEM((FULL + 2, NDEV, ROWS, LANES), BF16),
            pltpu.VMEM((C, LEV * LANES), BF16),
            pltpu.VMEM((C, C), BF16),
            pltpu.VMEM((C + 2 * QROWS, C), BF16),
            pltpu.VMEM((LEV, C, LANES), F32),
            pltpu.VMEM((C, LATENT * LANES), BF16),
            pltpu.VMEM((LANES, LATENT + 1, C), F32),
            pltpu.VMEM(surf_cells.shape, BF16),
            pltpu.VMEM(atmos_weight.shape, BF16),
            pltpu.VMEM(level_bias_table.shape, F32),
            pltpu.VMEM(query_matrix.shape, BF16),
            pltpu.VMEM(key_weight.shape, BF16),
            pltpu.VMEM(value_weight.shape, BF16),
            dma((FULL + 2,)),
            dma((8,)),
            dma((FULL + 1,)),
            dma((FULL + 1,)),
            dma((len(PIECES),)),
            dma((FULL + 1 + len(PIECES),)),
        ],
        compiler_params=pltpu.CompilerParams(
            collective_id=0, has_side_effects=True, vmem_limit_bytes=48 * 2**20
        ),
        name="exchange_and_encode",
    )(*[pltpu.with_memory_space_constraint(x, pltpu.HBM) for x in operands])
    return pl.pallas_call(
        finish,
        out_shape=jax.ShapeDtypeStruct((A, COLS, LATENT + 1, C), BF16),
        in_specs=[in_vmem] * 8,
        out_specs=in_hbm,
        scratch_shapes=[
            pltpu.VMEM((C, LATENT * LANES), BF16),
            pltpu.VMEM((LANES, LATENT + 1, C), F32),
            pltpu.VMEM((A, BLK, LATENT + 1, C), BF16),
            dma((4,)),
        ],
        compiler_params=pltpu.CompilerParams(vmem_limit_bytes=8 * 2**20),
        name="finish",
    )(*[pltpu.with_memory_space_constraint(x, pltpu.VMEM) for x in handed])


def solution(mesh):
    in_specs = (P(None, "lon", "lat"), P(), P(), P(), P(), P(), P(), P(), P())
    out_specs = P("lat", "lon", None, None)
    return jax.shard_map(shards, mesh=mesh, in_specs=in_specs, out_specs=out_specs, check_vma=False)
```

```python
import functools
import math

import jax
import jax.numpy as jnp
from jax import lax
from jax.experimental import pallas as pl
from jax.experimental.pallas import tpu as pltpu
from jax.sharding import PartitionSpec as P

C = 512
HEADS = 16
HEAD_CHANNELS = 32
K = 100
NSURF = 4
NATM = 5
LATENT = 3
LEV = 12
NDEV = 16
FPD = 4
ROWS = 400
A = 8
COLS = 90
LANES = 128
BLK = 16
FULL = 5
REST = 10
REST_ROWS = 256
KT = 25
QROWS = LATENT * HEADS
LAST = FULL - 1
OPENING = 80
PIECES = ((0, 208), (208, 400))
EARLY_LEVELS = 6
EARLY = 5 * BLK

MESH = pl.DeviceIdType.MESH
BF16 = jnp.bfloat16
F32 = jnp.float32


def far_first():
    offsets = [(dy, dz, dc) for dy in range(4) for dz in range(2) for dc in range(2)][1:]

    def rank(o):
        far = min(o[0], 4 - o[0]) + o[1]
        return -far, o[1] if far == 1 else 0

    return sorted(offsets, key=rank)


OFFSETS = far_first()
FAR = [o for o in OFFSETS if min(o[0], 4 - o[0]) + o[1] >= 2]
NEAR = [o for o in OFFSETS if o not in FAR]


def peer_of(me, offset):
    dy, dz, dc = offset
    y, z, c = me // 4, (me // 2) % 2, me % 2
    return ((y + dy) % 4) * 4 + ((z + dz) % 2) * 2 + (c + dc) % 2


def block_transpose(parts):
    lane = lax.broadcasted_iota(jnp.int32, parts[0].shape, 1)
    turned = [x if j == 0 else pltpu.roll(x, 8 * j, 1) for j, x in enumerate(parts)]
    held = [turned[-e % BLK] for e in range(BLK)]
    for s in (1, 2, 4, 8):
        mask = (lane & (8 * s)) != 0
        held = [jnp.where(mask, held[(e - s) % BLK], held[e]) for e in range(BLK)]
    return held


def mixture(terms, shares, out):
    for h in range(HEADS):
        rows = pl.ds(HEAD_CHANNELS * h, HEAD_CHANNELS)
        sums = [None] * LATENT
        for i, values in terms:
            held = [values(m)[rows, :] for m in range(LATENT)] if callable(values) else [values[rows, :]] * LATENT
            for m in range(LATENT):
                term = shares[i, pl.ds(m * HEADS + h, 1), :] * held[m]
                sums[m] = term if sums[m] is None else sums[m] + term
        for m in range(LATENT):
            out[rows, pl.ds(m * LANES, LANES)] = sums[m].astype(out.dtype)


def project(block, mix, wsurf, ow, lat, slots):
    contract = (((0,), (0,)), ((), ()))
    slots[:, 0, :] = lax.dot_general(block[...], wsurf[...], contract, preferred_element_type=F32)
    agg = lax.dot_general(mix[...], ow[...], contract, preferred_element_type=F32)
    for m in range(LATENT):
        slots[:, m + 1, :] = agg[m * LANES : (m + 1) * LANES] + lat[pl.ds(m, 1), :].astype(F32)


def kernel(
    fields_ref, surf_ref, atmos_ref, bias_ref, lat_ref, qm_ref, kw_ref, vw_ref, ow_ref,
    staged, vals, scores, part, last_surf, wsurf, ow_v, lat_v,
    inb, send, recv, xs, wat, wuv, biasb, mix, slots,
    surf_v, atmos_v, bias_v, qm_v, kw_v, vw_v,
    in_sem, w_sem, send_sem, recv_sem, piece_sem, self_sem,
):
    me = lax.axis_index("lat")
    rest_raw, rest_done = FULL, FULL + 1

    def load(c, n=BLK, start=0, stop=ROWS, sem=None):
        here, rows = pl.ds(BLK * c, n), pl.ds(start, stop - start)
        return pltpu.make_async_copy(
            fields_ref.at[here, rows], inb.at[here, rows], in_sem.at[c if sem is None else sem])

    load(0, stop=OPENING).start()
    barrier = pltpu.get_barrier_semaphore()
    for o in OFFSETS:
        pl.semaphore_signal(barrier, inc=1, device_id={"lat": peer_of(me, o)}, device_id_type=MESH)
    load(0, start=OPENING, sem=FULL + 1).start()
    def unturn(e, y):
        return y if e == 0 else pltpu.roll(y, LANES - 8 * e, 1)

    def shuffle_full(c, straight=False, start=0, stop=ROWS):
        def tile(t, carry):
            rows = pl.ds(pl.multiple_of(16 * t, 16), 16)
            parts = [inb[BLK * c + j, rows, :] for j in range(BLK)]
            for e, y in enumerate(block_transpose(parts)):
                send[c, e, rows, :] = unturn(e, y) if straight else y
            return carry
        lax.fori_loop(start // 16, stop // 16, tile, 0, unroll=5)

    def rest_group(q, g, count):
        parts = []
        for j in range(BLK):
            t, b = divmod(BLK * g + j, REST) if j < count else (0, j - count)
            rows = pl.ds(pl.multiple_of(128 * q + 16 * t, 16), 16)
            parts.append(inb[BLK * FULL + b, rows, :])
        rows = pl.ds(pl.multiple_of(80 * q + 16 * g, 16), 16)
        for e, y in enumerate(block_transpose(parts)):
            send[FULL, e, rows, :] = unturn(e, y)

    def shuffle_rest():
        def five(q, carry):
            for g in range(5):
                rest_group(q, g, BLK)
            return carry
        lax.fori_loop(0, 3, five, 0)
        rest_group(3, 0, REST)

    def own(c, start, stop, sem):
        rows = pl.ds(start, stop - start)
        return pltpu.make_async_copy(send.at[c, me, rows], recv.at[c, me, rows], sem)

    def ship(c, start, stop, sem, own_sem, offsets=OFFSETS):
        rows = pl.ds(start, stop - start)
        for o in offsets:
            d = peer_of(me, o)
            pltpu.make_async_remote_copy(
                src_ref=send.at[c, d, rows], dst_ref=recv.at[c, me, rows],
                send_sem=send_sem.at[c], recv_sem=sem,
                device_id={"lat": d}, device_id_type=MESH,
            ).start()
        if own_sem is not None:
            own(c, start, stop, own_sem).start()

    def ship_whole(c, rows):
        ship(c, 0, rows, recv_sem.at[c], self_sem.at[c])

    load(0, stop=OPENING).wait()
    shuffle_full(0, stop=OPENING)
    pl.semaphore_wait(barrier, NDEV - 1)
    ship(0, 0, OPENING, recv_sem.at[0], self_sem.at[0])
    for c in range(1, FULL):
        load(c).start()
    load(FULL, REST).start()
    load(0, start=OPENING, sem=FULL + 1).wait()
    shuffle_full(0, start=OPENING)
    ship(0, OPENING, ROWS, recv_sem.at[0], self_sem.at[0])
    weight_loads = []
    for i, (src, dst) in enumerate((
        (qm_ref, qm_v), (lat_ref, lat_v), (kw_ref, kw_v), (vw_ref, vw_v), (atmos_ref, atmos_v),
        (surf_ref, surf_v), (bias_ref, bias_v), (ow_ref, ow_v),
    )):
        weight_loads.append(pltpu.make_async_copy(src, dst, w_sem.at[i]))
        weight_loads[-1].start()

    def send_next(c, carry):
        load(c).wait()
        shuffle_full(c)
        ship_whole(c, ROWS)
        return carry
    lax.fori_loop(1, LAST, send_next, 0)
    load(FULL, REST).wait()
    shuffle_rest()
    ship_whole(FULL, REST_ROWS)
    load(LAST).wait()
    shuffle_full(LAST, straight=True)
    for o in FAR:
        for i, (start, stop) in enumerate(PIECES):
            ship(LAST, start, stop, piece_sem.at[i], None, [o])
    for i, (start, stop) in enumerate(PIECES):
        ship(LAST, start, stop, piece_sem.at[i], self_sem.at[FULL + 1 + i], NEAR)

    for w in weight_loads:
        w.wait()
    queries = jnp.dot(lat_v[...], qm_v[...], preferred_element_type=F32).astype(BF16).astype(F32)
    channel_head = lax.broadcasted_iota(jnp.int32, (HEADS, C), 1) // HEAD_CHANNELS
    own_head = channel_head == lax.broadcasted_iota(jnp.int32, (HEADS, C), 0)
    spread = jnp.concatenate(
        [jnp.where(own_head, jnp.broadcast_to(queries[m : m + 1], (HEADS, C)), 0.0) for m in range(LATENT)],
        axis=0,
    ).astype(BF16)
    score_w = lax.dot_general(
        spread, kw_v[...], (((1,), (1,)), ((), ())), preferred_element_type=F32
    ) * (1.0 / math.sqrt(HEAD_CHANNELS))
    high = score_w.astype(BF16)
    wuv[pl.ds(0, QROWS), :] = high
    wuv[pl.ds(QROWS, QROWS), :] = (score_w - high.astype(F32)).astype(BF16)
    wuv[pl.ds(2 * QROWS, C), :] = vw_v[...].astype(F32).T.astype(BF16)
    stacked = jnp.concatenate(
        [atmos_v[v].astype(F32) for v in range(NATM)] + [jnp.zeros((C - NATM * K, C), F32)], axis=0
    )
    wat[...] = stacked.T.astype(BF16)
    wsurf[...] = jnp.concatenate([surf_v[:, f, :].astype(F32) for f in range(NSURF)], axis=0).astype(BF16)

    for n in range(LEV):
        l = 4 * (n % 3) + n // 3
        biasb[n] = jnp.broadcast_to(bias_v[pl.ds(l, 1), :], (LANES, C)).T
    xs[pl.ds(C - 16, 16), :] = jnp.zeros((16, LEV * LANES), BF16)

    def unpack(s, carry):
        lane = lax.broadcasted_iota(jnp.int32, (16, LANES), 1)
        for t in range(KT):
            g, off = divmod(8 * REST * t, LANES)
            x = recv[rest_raw, s, 16 * g : 16 * g + 16, :]
            if off:
                x = pltpu.roll(x, LANES - off, 1)
            if off + 8 * REST > LANES:
                y = pltpu.roll(recv[rest_raw, s, 16 * g + 16 : 16 * g + 32, :], LANES - off, 1)
                x = jnp.where(lane < LANES - off, x, y)
            recv[rest_done, s, 16 * t : 16 * t + 16, :] = x
        return carry

    def gather(place, j):
        for s in range(1, NDEV):
            v, g = divmod(s - 1, 3)
            xs[pl.ds(K * v, K), pl.ds((3 * j + g) * LANES, LANES)] = recv[place, s, pl.ds(K * j, K), :]

    def embed(first, count):
        cols = pl.ds(first * LANES, count * LANES)
        levels = jnp.dot(wat[...], xs[:, cols], preferred_element_type=F32)
        levels = levels + jnp.concatenate([biasb[first + i] for i in range(count)], axis=1)
        centred = levels - jnp.sum(levels, axis=0, keepdims=True) * (1.0 / C)
        var = jnp.sum(centred * centred, axis=0, keepdims=True) * (1.0 / C)
        xs[:, cols] = (centred * lax.rsqrt(var + 1e-5)).astype(BF16)

    def attend(first, count):
        got = jnp.dot(wuv[...], xs[:, pl.ds(first * LANES, count * LANES)], preferred_element_type=F32)
        for i in range(count):
            part = got[:, i * LANES : (i + 1) * LANES]
            scores[first + i] = part[:QROWS] + part[QROWS : 2 * QROWS]
            vals[first + i] = part[2 * QROWS :].astype(BF16).astype(F32)

    def softmax():
        top = scores[0]
        for l in range(1, LEV):
            top = jnp.maximum(top, scores[l])
        total = jnp.zeros((QROWS, LANES), F32)
        for l in range(LEV):
            e = jnp.exp(scores[l] - top)
            scores[l] = e
            total = total + e
        for l in range(LEV):
            scores[l] = (scores[l] / total).astype(BF16).astype(F32)

    def lay_out(t, turn):
        def move(j, carry):
            start = pl.multiple_of(A * lax.rem(j + turn, BLK), A)
            for a in range(A):
                staged[a, BLK * t + j] = slots[start + a].astype(BF16)
            return carry
        lax.fori_loop(0, BLK, move, 0, unroll=2)

    def arrived(c, start, stop, sem, own_sem):
        whole = recv.at[c, pl.ds(0, NDEV - 1), pl.ds(start, stop - start)]
        pltpu.make_async_copy(whole, whole, sem).wait()
        own(c, start, stop, own_sem).wait()

    def process(t, carry):
        is_rest = t // LAST
        place = t + is_rest * (rest_done - LAST)

        @pl.when(t < LAST)
        def _():
            arrived(t, 0, ROWS, recv_sem.at[t], self_sem.at[t])

        @pl.when(t == LAST)
        def _():
            arrived(FULL, 0, REST_ROWS, recv_sem.at[FULL], self_sem.at[FULL])
            lax.fori_loop(0, NDEV, unpack, 0, unroll=2)

        for j in range(FPD):
            gather(place, j)
        for p in range(LEV // 2):
            embed(2 * p, 2)
        for p in range(LEV // 2):
            attend(2 * p, 2)
        softmax()
        mixture([(l, vals.at[l]) for l in range(LEV)], scores, mix)
        project(recv.at[place, 0], mix, wsurf, ow_v, lat_v, slots)
        lay_out(t, me * (1 - is_rest))
        return carry
    lax.fori_loop(0, FULL, process, 0)

    def piece(i):
        start, stop = PIECES[i]
        arrived(LAST, start, stop, piece_sem.at[i], self_sem.at[FULL + 1 + i])
        rows = pl.ds(start, stop - start)
        last_surf[rows, :] = recv[LAST, 0, rows, :]

    early = EARLY_LEVELS
    piece(0)
    for j in range(2):
        gather(LAST, j)
    for p in range(0, early, 2):
        embed(p, 2)
    for p in range(0, early, 2):
        attend(p, 2)
    top = scores[0]
    for l in range(1, early):
        top = jnp.maximum(top, scores[l])
    total = jnp.zeros((QROWS, LANES), F32)
    for l in range(early):
        e = jnp.exp(scores[l] - top)
        scores[l] = e
        total = total + e
    mixture([(l, vals.at[l]) for l in range(early)], scores, part)
    scores[0] = top
    scores[1] = total

    piece(1)
    for j in range(2, FPD):
        gather(LAST, j)
    for p in range(early, LEV, 2):
        embed(p, 2)
    for p in range(early, LEV, 2):
        attend(p, 2)
    last = [scores[l] for l in range(early, LEV)]
    top = scores[0]
    for x in last:
        top = jnp.maximum(top, x)
    last = [jnp.exp(x - top) for x in last]
    scale = jnp.exp(scores[0] - top)
    share = 1.0 / (sum(last) + scale * scores[1])
    scores[0] = scale * share
    for i, e in enumerate(last):
        scores[early + i] = e * share

    for c in range(FULL + 1):
        whole = send.at[c, pl.ds(0, NDEV - 1), pl.ds(0, ROWS if c < FULL else REST_ROWS)]
        pltpu.make_async_copy(whole, whole, send_sem.at[c]).wait()


def finish(staged, vals, scores, part, last_surf, wsurf, ow, lat, out_ref, mix, slots, outb, sem):
    ahead = BLK * LAST
    writes = [
        pltpu.make_async_copy(staged.at[:, pl.ds(0, ahead)], out_ref.at[:, pl.ds(0, ahead)], sem.at[0]),
        pltpu.make_async_copy(staged.at[:, pl.ds(ahead, REST)], out_ref.at[:, pl.ds(BLK * FULL, REST)], sem.at[1]),
    ]
    for write in writes:
        write.start()
    mixture([(0, lambda m: part.at[:, pl.ds(m * LANES, LANES)])] + [(l, vals.at[l]) for l in range(EARLY_LEVELS, LEV)], scores, mix)
    project(last_surf, mix, wsurf, ow, lat, slots)

    def move(j, carry):
        start = pl.multiple_of(A * j, A)
        for a in range(A):
            outb[a, j] = slots[start + a].astype(BF16)
        return carry
    part_cols = BLK // 4
    for i in range(4):
        lax.fori_loop(part_cols * i, part_cols * (i + 1), move, 0, unroll=4)
        writes.append(pltpu.make_async_copy(
            outb.at[:, pl.ds(part_cols * i, part_cols)],
            out_ref.at[:, pl.ds(ahead + part_cols * i, part_cols)], sem.at[2 + i]))
        writes[-1].start()
    for write in writes:
        write.wait()


def shards(fields, surf_weight, atmos_weight, level_bias_table, latents, query_matrix, key_weight, value_weight, out_weight):
    by_token = jnp.transpose(fields, (1, 2, 0))
    surf_cells = jnp.transpose(surf_weight, (1, 0, 2))
    operands = (
        by_token, surf_cells, atmos_weight, level_bias_table, latents,
        query_matrix, key_weight, value_weight, out_weight,
    )
    in_hbm = pl.BlockSpec(memory_space=pl.ANY)
    in_vmem = pl.BlockSpec(memory_space=pltpu.VMEM)
    dma = pltpu.SemaphoreType.DMA
    handed = pl.pallas_call(
        kernel,
        out_shape=[
            pltpu.VMEM((A, EARLY, LATENT + 1, C), BF16),
            pltpu.VMEM((LEV, C, LANES), F32),
            pltpu.VMEM((LEV, QROWS, LANES), F32),
            pltpu.VMEM((C, LATENT * LANES), F32),
            pltpu.VMEM((ROWS, LANES), BF16),
            pltpu.VMEM((NSURF * K, C), BF16),
            pltpu.VMEM((C, C), BF16),
            pltpu.VMEM((LATENT, C), BF16),
        ],
        in_specs=[in_hbm] * 9,
        out_specs=[in_vmem] * 8,
        scratch_shapes=[
            pltpu.VMEM((COLS, ROWS, LANES), BF16),
            pltpu.VMEM((FULL + 1, NDEV, ROWS, LANES), BF16),
            pltpu.VMEM((FULL + 2, NDEV, ROWS, LANES), BF16),
            pltpu.VMEM((C, LEV * LANES), BF16),
            pltpu.VMEM((C, C), BF16),
            pltpu.VMEM((C + 2 * QROWS, C), BF16),
            pltpu.VMEM((LEV, C, LANES), F32),
            pltpu.VMEM((C, LATENT * LANES), BF16),
            pltpu.VMEM((LANES, LATENT + 1, C), F32),
            pltpu.VMEM(surf_cells.shape, BF16),
            pltpu.VMEM(atmos_weight.shape, BF16),
            pltpu.VMEM(level_bias_table.shape, F32),
            pltpu.VMEM(query_matrix.shape, BF16),
            pltpu.VMEM(key_weight.shape, BF16),
            pltpu.VMEM(value_weight.shape, BF16),
            dma((FULL + 2,)),
            dma((8,)),
            dma((FULL + 1,)),
            dma((FULL + 1,)),
            dma((len(PIECES),)),
            dma((FULL + 1 + len(PIECES),)),
        ],
        compiler_params=pltpu.CompilerParams(
            collective_id=0, has_side_effects=True, vmem_limit_bytes=48 * 2**20
        ),
        name="exchange_and_encode",
    )(*[pltpu.with_memory_space_constraint(x, pltpu.HBM) for x in operands])
    return pl.pallas_call(
        finish,
        out_shape=jax.ShapeDtypeStruct((A, COLS, LATENT + 1, C), BF16),
        in_specs=[in_vmem] * 8,
        out_specs=in_hbm,
        scratch_shapes=[
            pltpu.VMEM((C, LATENT * LANES), BF16),
            pltpu.VMEM((LANES, LATENT + 1, C), F32),
            pltpu.VMEM((A, BLK, LATENT + 1, C), BF16),
            dma((6,)),
        ],
        compiler_params=pltpu.CompilerParams(vmem_limit_bytes=8 * 2**20),
        name="finish",
    )(*[pltpu.with_memory_space_constraint(x, pltpu.VMEM) for x in handed])


def solution(mesh):
    in_specs = (P(None, "lon", "lat"), P(), P(), P(), P(), P(), P(), P(), P())
    out_specs = P("lat", "lon", None, None)
    return jax.shard_map(shards, mesh=mesh, in_specs=in_specs, out_specs=out_specs, check_vma=False)
```

```python
import functools
import math

import jax
import jax.numpy as jnp
from jax import lax
from jax.experimental import pallas as pl
from jax.experimental.pallas import tpu as pltpu
from jax.sharding import PartitionSpec as P

C = 512
HEADS = 16
HEAD_CHANNELS = 32
K = 100
NSURF = 4
NATM = 5
LATENT = 3
LEV = 12
NDEV = 16
FPD = 4
ROWS = 400
A = 8
COLS = 90
LANES = 128
BLK = 16
FULL = 5
REST = 10
REST_ROWS = 256
KT = 25
QROWS = LATENT * HEADS
LAST = FULL - 1
OPENING = 80
PIECES = ((0, 208), (208, 400))
EARLY_LEVELS = 6
EARLY = 5 * BLK

MESH = pl.DeviceIdType.MESH
BF16 = jnp.bfloat16
F32 = jnp.float32


def far_first():
    offsets = [(dy, dz, dc) for dy in range(4) for dz in range(2) for dc in range(2)][1:]
    return sorted(offsets, key=lambda o: -(min(o[0], 4 - o[0]) + o[1]))


OFFSETS = far_first()
FAR = [(0, 0, 1)] + [o for o in OFFSETS if min(o[0], 4 - o[0]) + o[1] >= 2]
NEAR = [o for o in OFFSETS if o not in FAR]


def peer_of(me, offset):
    dy, dz, dc = offset
    y, z, c = me // 4, (me // 2) % 2, me % 2
    return ((y + dy) % 4) * 4 + ((z + dz) % 2) * 2 + (c + dc) % 2


def block_transpose(parts):
    lane = lax.broadcasted_iota(jnp.int32, parts[0].shape, 1)
    turned = [x if j == 0 else pltpu.roll(x, 8 * j, 1) for j, x in enumerate(parts)]
    held = [turned[-e % BLK] for e in range(BLK)]
    for s in (1, 2, 4, 8):
        mask = (lane & (8 * s)) != 0
        held = [jnp.where(mask, held[(e - s) % BLK], held[e]) for e in range(BLK)]
    return held


def mixture(terms, shares, out):
    for h in range(HEADS):
        rows = pl.ds(HEAD_CHANNELS * h, HEAD_CHANNELS)
        sums = [None] * LATENT
        for i, values in terms:
            held = [values(m)[rows, :] for m in range(LATENT)] if callable(values) else [values[rows, :]] * LATENT
            for m in range(LATENT):
                term = shares[i, pl.ds(m * HEADS + h, 1), :] * held[m]
                sums[m] = term if sums[m] is None else sums[m] + term
        for m in range(LATENT):
            out[rows, pl.ds(m * LANES, LANES)] = sums[m].astype(out.dtype)


def project(block, mix, wsurf, ow, lat, slots):
    contract = (((0,), (0,)), ((), ()))
    slots[:, 0, :] = lax.dot_general(block[...], wsurf[...], contract, preferred_element_type=F32)
    agg = lax.dot_general(mix[...], ow[...], contract, preferred_element_type=F32)
    for m in range(LATENT):
        slots[:, m + 1, :] = agg[m * LANES : (m + 1) * LANES] + lat[pl.ds(m, 1), :].astype(F32)


def kernel(
    fields_ref, surf_ref, atmos_ref, bias_ref, lat_ref, qm_ref, kw_ref, vw_ref, ow_ref,
    staged, vals, scores, part, last_surf, wsurf, ow_v, lat_v,
    inb, send, recv, xs, wat, wuv, biasb, mix, slots,
    surf_v, atmos_v, bias_v, qm_v, kw_v, vw_v,
    in_sem, w_sem, send_sem, recv_sem, piece_sem, self_sem,
):
    me = lax.axis_index("lat")
    rest_raw, rest_done = FULL, FULL + 1

    def load(c, n=BLK, start=0, stop=ROWS, sem=None):
        here, rows = pl.ds(BLK * c, n), pl.ds(start, stop - start)
        return pltpu.make_async_copy(
            fields_ref.at[here, rows], inb.at[here, rows], in_sem.at[c if sem is None else sem])

    load(0, stop=OPENING).start()
    barrier = pltpu.get_barrier_semaphore()
    for o in OFFSETS:
        pl.semaphore_signal(barrier, inc=1, device_id={"lat": peer_of(me, o)}, device_id_type=MESH)
    load(0, start=OPENING, sem=FULL + 1).start()
    def unturn(e, y):
        return y if e == 0 else pltpu.roll(y, LANES - 8 * e, 1)

    def shuffle_full(c, straight=False, start=0, stop=ROWS):
        def tile(t, carry):
            rows = pl.ds(pl.multiple_of(16 * t, 16), 16)
            parts = [inb[BLK * c + j, rows, :] for j in range(BLK)]
            for e, y in enumerate(block_transpose(parts)):
                send[c, e, rows, :] = unturn(e, y) if straight else y
            return carry
        lax.fori_loop(start // 16, stop // 16, tile, 0, unroll=5)

    def rest_group(q, g, count):
        parts = []
        for j in range(BLK):
            t, b = divmod(BLK * g + j, REST) if j < count else (0, j - count)
            rows = pl.ds(pl.multiple_of(128 * q + 16 * t, 16), 16)
            parts.append(inb[BLK * FULL + b, rows, :])
        rows = pl.ds(pl.multiple_of(80 * q + 16 * g, 16), 16)
        for e, y in enumerate(block_transpose(parts)):
            send[FULL, e, rows, :] = unturn(e, y)

    def shuffle_rest():
        def five(q, carry):
            for g in range(5):
                rest_group(q, g, BLK)
            return carry
        lax.fori_loop(0, 3, five, 0)
        rest_group(3, 0, REST)

    def own(c, start, stop, sem):
        rows = pl.ds(start, stop - start)
        return pltpu.make_async_copy(send.at[c, me, rows], recv.at[c, me, rows], sem)

    def ship(c, start, stop, sem, own_sem, offsets=OFFSETS):
        rows = pl.ds(start, stop - start)
        for o in offsets:
            d = peer_of(me, o)
            pltpu.make_async_remote_copy(
                src_ref=send.at[c, d, rows], dst_ref=recv.at[c, me, rows],
                send_sem=send_sem.at[c], recv_sem=sem,
                device_id={"lat": d}, device_id_type=MESH,
            ).start()
        if own_sem is not None:
            own(c, start, stop, own_sem).start()

    def ship_whole(c, rows):
        ship(c, 0, rows, recv_sem.at[c], self_sem.at[c])

    load(0, stop=OPENING).wait()
    shuffle_full(0, stop=OPENING)
    pl.semaphore_wait(barrier, NDEV - 1)
    ship(0, 0, OPENING, recv_sem.at[0], self_sem.at[0])
    for c in range(1, FULL):
        load(c).start()
    load(FULL, REST).start()
    load(0, start=OPENING, sem=FULL + 1).wait()
    shuffle_full(0, start=OPENING)
    ship(0, OPENING, ROWS, recv_sem.at[0], self_sem.at[0])
    weight_loads = []
    for i, (src, dst) in enumerate((
        (qm_ref, qm_v), (lat_ref, lat_v), (kw_ref, kw_v), (vw_ref, vw_v), (atmos_ref, atmos_v),
        (surf_ref, surf_v), (bias_ref, bias_v), (ow_ref, ow_v),
    )):
        weight_loads.append(pltpu.make_async_copy(src, dst, w_sem.at[i]))
        weight_loads[-1].start()

    def send_next(c, carry):
        load(c).wait()
        shuffle_full(c)
        ship_whole(c, ROWS)
        return carry
    lax.fori_loop(1, LAST, send_next, 0)
    load(FULL, REST).wait()
    shuffle_rest()
    ship_whole(FULL, REST_ROWS)
    load(LAST).wait()
    shuffle_full(LAST, straight=True)
    for o in FAR:
        for i, (start, stop) in enumerate(PIECES):
            ship(LAST, start, stop, piece_sem.at[i], None, [o])
    for i, (start, stop) in enumerate(PIECES):
        ship(LAST, start, stop, piece_sem.at[i], self_sem.at[FULL + 1 + i], NEAR)

    for w in weight_loads:
        w.wait()
    queries = jnp.dot(lat_v[...], qm_v[...], preferred_element_type=F32).astype(BF16).astype(F32)
    channel_head = lax.broadcasted_iota(jnp.int32, (HEADS, C), 1) // HEAD_CHANNELS
    own_head = channel_head == lax.broadcasted_iota(jnp.int32, (HEADS, C), 0)
    spread = jnp.concatenate(
        [jnp.where(own_head, jnp.broadcast_to(queries[m : m + 1], (HEADS, C)), 0.0) for m in range(LATENT)],
        axis=0,
    ).astype(BF16)
    score_w = lax.dot_general(
        spread, kw_v[...], (((1,), (1,)), ((), ())), preferred_element_type=F32
    ) * (1.0 / math.sqrt(HEAD_CHANNELS))
    high = score_w.astype(BF16)
    wuv[pl.ds(0, QROWS), :] = high
    wuv[pl.ds(QROWS, QROWS), :] = (score_w - high.astype(F32)).astype(BF16)
    wuv[pl.ds(2 * QROWS, C), :] = vw_v[...].astype(F32).T.astype(BF16)
    stacked = jnp.concatenate(
        [atmos_v[v].astype(F32) for v in range(NATM)] + [jnp.zeros((C - NATM * K, C), F32)], axis=0
    )
    wat[...] = stacked.T.astype(BF16)
    wsurf[...] = jnp.concatenate([surf_v[:, f, :].astype(F32) for f in range(NSURF)], axis=0).astype(BF16)

    for n in range(LEV):
        l = 4 * (n % 3) + n // 3
        biasb[n] = jnp.broadcast_to(bias_v[pl.ds(l, 1), :], (LANES, C)).T
    xs[pl.ds(C - 16, 16), :] = jnp.zeros((16, LEV * LANES), BF16)

    def unpack(s, carry):
        lane = lax.broadcasted_iota(jnp.int32, (16, LANES), 1)
        for t in range(KT):
            g, off = divmod(8 * REST * t, LANES)
            x = recv[rest_raw, s, 16 * g : 16 * g + 16, :]
            if off:
                x = pltpu.roll(x, LANES - off, 1)
            if off + 8 * REST > LANES:
                y = pltpu.roll(recv[rest_raw, s, 16 * g + 16 : 16 * g + 32, :], LANES - off, 1)
                x = jnp.where(lane < LANES - off, x, y)
            recv[rest_done, s, 16 * t : 16 * t + 16, :] = x
        return carry

    def gather(place, j):
        for s in range(1, NDEV):
            v, g = divmod(s - 1, 3)
            xs[pl.ds(K * v, K), pl.ds((3 * j + g) * LANES, LANES)] = recv[place, s, pl.ds(K * j, K), :]

    def embed(first, count):
        cols = pl.ds(first * LANES, count * LANES)
        levels = jnp.dot(wat[...], xs[:, cols], preferred_element_type=F32)
        levels = levels + jnp.concatenate([biasb[first + i] for i in range(count)], axis=1)
        centred = levels - jnp.sum(levels, axis=0, keepdims=True) * (1.0 / C)
        var = jnp.sum(centred * centred, axis=0, keepdims=True) * (1.0 / C)
        xs[:, cols] = (centred * lax.rsqrt(var + 1e-5)).astype(BF16)

    def attend(first, count):
        got = jnp.dot(wuv[...], xs[:, pl.ds(first * LANES, count * LANES)], preferred_element_type=F32)
        for i in range(count):
            part = got[:, i * LANES : (i + 1) * LANES]
            scores[first + i] = part[:QROWS] + part[QROWS : 2 * QROWS]
            vals[first + i] = part[2 * QROWS :].astype(BF16).astype(F32)

    def softmax():
        top = scores[0]
        for l in range(1, LEV):
            top = jnp.maximum(top, scores[l])
        total = jnp.zeros((QROWS, LANES), F32)
        for l in range(LEV):
            e = jnp.exp(scores[l] - top)
            scores[l] = e
            total = total + e
        for l in range(LEV):
            scores[l] = (scores[l] / total).astype(BF16).astype(F32)

    def lay_out(t, turn):
        def move(j, carry):
            start = pl.multiple_of(A * lax.rem(j + turn, BLK), A)
            for a in range(A):
                staged[a, BLK * t + j] = slots[start + a].astype(BF16)
            return carry
        lax.fori_loop(0, BLK, move, 0, unroll=2)

    def arrived(c, start, stop, sem, own_sem):
        whole = recv.at[c, pl.ds(0, NDEV - 1), pl.ds(start, stop - start)]
        pltpu.make_async_copy(whole, whole, sem).wait()
        own(c, start, stop, own_sem).wait()

    def process(t, carry):
        is_rest = t // LAST
        place = t + is_rest * (rest_done - LAST)

        @pl.when(t < LAST)
        def _():
            arrived(t, 0, ROWS, recv_sem.at[t], self_sem.at[t])

        @pl.when(t == LAST)
        def _():
            arrived(FULL, 0, REST_ROWS, recv_sem.at[FULL], self_sem.at[FULL])
            lax.fori_loop(0, NDEV, unpack, 0, unroll=2)

        for j in range(FPD):
            gather(place, j)
        for p in range(LEV // 2):
            embed(2 * p, 2)
        for p in range(LEV // 2):
            attend(2 * p, 2)
        softmax()
        mixture([(l, vals.at[l]) for l in range(LEV)], scores, mix)
        project(recv.at[place, 0], mix, wsurf, ow_v, lat_v, slots)
        lay_out(t, me * (1 - is_rest))
        return carry
    lax.fori_loop(0, FULL, process, 0)

    def piece(i):
        start, stop = PIECES[i]
        arrived(LAST, start, stop, piece_sem.at[i], self_sem.at[FULL + 1 + i])
        rows = pl.ds(start, stop - start)
        last_surf[rows, :] = recv[LAST, 0, rows, :]

    early = EARLY_LEVELS
    piece(0)
    for j in range(2):
        gather(LAST, j)
    for p in range(0, early, 2):
        embed(p, 2)
    for p in range(0, early, 2):
        attend(p, 2)
    top = scores[0]
    for l in range(1, early):
        top = jnp.maximum(top, scores[l])
    total = jnp.zeros((QROWS, LANES), F32)
    for l in range(early):
        e = jnp.exp(scores[l] - top)
        scores[l] = e
        total = total + e
    mixture([(l, vals.at[l]) for l in range(early)], scores, part)
    scores[0] = top
    scores[1] = total

    piece(1)
    for j in range(2, FPD):
        gather(LAST, j)
    for p in range(early, LEV, 2):
        embed(p, 2)
    for p in range(early, LEV, 2):
        attend(p, 2)
    last = [scores[l] for l in range(early, LEV)]
    top = scores[0]
    for x in last:
        top = jnp.maximum(top, x)
    last = [jnp.exp(x - top) for x in last]
    scale = jnp.exp(scores[0] - top)
    share = 1.0 / (sum(last) + scale * scores[1])
    scores[0] = scale * share
    for i, e in enumerate(last):
        scores[early + i] = e * share

    for c in range(FULL + 1):
        whole = send.at[c, pl.ds(0, NDEV - 1), pl.ds(0, ROWS if c < FULL else REST_ROWS)]
        pltpu.make_async_copy(whole, whole, send_sem.at[c]).wait()


def finish(staged, vals, scores, part, last_surf, wsurf, ow, lat, out_ref, mix, slots, outb, sem):
    ahead = BLK * LAST
    writes = [
        pltpu.make_async_copy(staged.at[:, pl.ds(0, ahead)], out_ref.at[:, pl.ds(0, ahead)], sem.at[0]),
        pltpu.make_async_copy(staged.at[:, pl.ds(ahead, REST)], out_ref.at[:, pl.ds(BLK * FULL, REST)], sem.at[1]),
    ]
    for write in writes:
        write.start()
    mixture([(0, lambda m: part.at[:, pl.ds(m * LANES, LANES)])] + [(l, vals.at[l]) for l in range(EARLY_LEVELS, LEV)], scores, mix)
    project(last_surf, mix, wsurf, ow, lat, slots)

    def move(j, carry):
        start = pl.multiple_of(A * j, A)
        for a in range(A):
            outb[a, j] = slots[start + a].astype(BF16)
        return carry
    half = BLK // 2
    for i in range(2):
        lax.fori_loop(half * i, half * (i + 1), move, 0, unroll=4)
        writes.append(pltpu.make_async_copy(
            outb.at[:, pl.ds(half * i, half)], out_ref.at[:, pl.ds(ahead + half * i, half)], sem.at[2 + i]))
        writes[-1].start()
    for write in writes:
        write.wait()


def shards(fields, surf_weight, atmos_weight, level_bias_table, latents, query_matrix, key_weight, value_weight, out_weight):
    by_token = jnp.transpose(fields, (1, 2, 0))
    surf_cells = jnp.transpose(surf_weight, (1, 0, 2))
    operands = (
        by_token, surf_cells, atmos_weight, level_bias_table, latents,
        query_matrix, key_weight, value_weight, out_weight,
    )
    in_hbm = pl.BlockSpec(memory_space=pl.ANY)
    in_vmem = pl.BlockSpec(memory_space=pltpu.VMEM)
    dma = pltpu.SemaphoreType.DMA
    handed = pl.pallas_call(
        kernel,
        out_shape=[
            pltpu.VMEM((A, EARLY, LATENT + 1, C), BF16),
            pltpu.VMEM((LEV, C, LANES), F32),
            pltpu.VMEM((LEV, QROWS, LANES), F32),
            pltpu.VMEM((C, LATENT * LANES), F32),
            pltpu.VMEM((ROWS, LANES), BF16),
            pltpu.VMEM((NSURF * K, C), BF16),
            pltpu.VMEM((C, C), BF16),
            pltpu.VMEM((LATENT, C), BF16),
        ],
        in_specs=[in_hbm] * 9,
        out_specs=[in_vmem] * 8,
        scratch_shapes=[
            pltpu.VMEM((COLS, ROWS, LANES), BF16),
            pltpu.VMEM((FULL + 1, NDEV, ROWS, LANES), BF16),
            pltpu.VMEM((FULL + 2, NDEV, ROWS, LANES), BF16),
            pltpu.VMEM((C, LEV * LANES), BF16),
            pltpu.VMEM((C, C), BF16),
            pltpu.VMEM((C + 2 * QROWS, C), BF16),
            pltpu.VMEM((LEV, C, LANES), F32),
            pltpu.VMEM((C, LATENT * LANES), BF16),
            pltpu.VMEM((LANES, LATENT + 1, C), F32),
            pltpu.VMEM(surf_cells.shape, BF16),
            pltpu.VMEM(atmos_weight.shape, BF16),
            pltpu.VMEM(level_bias_table.shape, F32),
            pltpu.VMEM(query_matrix.shape, BF16),
            pltpu.VMEM(key_weight.shape, BF16),
            pltpu.VMEM(value_weight.shape, BF16),
            dma((FULL + 2,)),
            dma((8,)),
            dma((FULL + 1,)),
            dma((FULL + 1,)),
            dma((len(PIECES),)),
            dma((FULL + 1 + len(PIECES),)),
        ],
        compiler_params=pltpu.CompilerParams(
            collective_id=0, has_side_effects=True, vmem_limit_bytes=48 * 2**20
        ),
        name="exchange_and_encode",
    )(*[pltpu.with_memory_space_constraint(x, pltpu.HBM) for x in operands])
    return pl.pallas_call(
        finish,
        out_shape=jax.ShapeDtypeStruct((A, COLS, LATENT + 1, C), BF16),
        in_specs=[in_vmem] * 8,
        out_specs=in_hbm,
        scratch_shapes=[
            pltpu.VMEM((C, LATENT * LANES), BF16),
            pltpu.VMEM((LANES, LATENT + 1, C), F32),
            pltpu.VMEM((A, BLK, LATENT + 1, C), BF16),
            dma((4,)),
        ],
        compiler_params=pltpu.CompilerParams(vmem_limit_bytes=8 * 2**20),
        name="finish",
    )(*[pltpu.with_memory_space_constraint(x, pltpu.VMEM) for x in handed])


def solution(mesh):
    in_specs = (P(None, "lon", "lat"), P(), P(), P(), P(), P(), P(), P(), P())
    out_specs = P("lat", "lon", None, None)
    return jax.shard_map(shards, mesh=mesh, in_specs=in_specs, out_specs=out_specs, check_vma=False)
```
